32 devices in a mesh: grp: 4 (over z), dp: 8 (over y, x, core).
Axes of the slice: x: 2, y: 2, z: 4, core: 2. Of those that a mesh axis runs over, the one named last changes fastest.
Arguments:
- tokens: bfloat16 [32, 1024, 768], P(('grp', 'dp')), may hold values from -6 to 6
- grad_out: bfloat16 [32, 1024, 768], P(('grp', 'dp')), may hold values from -6 to 6
- lengths: int32 [32], P(('grp', 'dp')), may hold values from 32 to 1024, as said below
- task_of: int32 [32], P(('grp', 'dp')), may hold values from 0 to 15
- task_tokens: int32 [16], replicated, may hold values from 256 to 4096
- w_qkv: bfloat16 [768, 2304], P('dp'), may hold values from -0.21875 to 0.21875
- w_out: bfloat16 [768, 768], P('dp'), may hold values from -1.75 to 1.75
- w_up: bfloat16 [768, 3072], P('dp'), may hold values from -0.21875 to 0.21875
- w_down: bfloat16 [3072, 768], P('dp'), may hold values from -0.109375 to 0.109375
- bias_q: bfloat16 [768], P('dp'), may hold values from -3 to 3
- bias_v: bfloat16 [768], P('dp'), may hold values from -3 to 3
- bias_out: bfloat16 [768], P('dp'), may hold values from -3 to 3
- bias_up: bfloat16 [3072], P('dp'), may hold values from -3 to 3
- bias_down: bfloat16 [768], P('dp'), may hold values from -3 to 3
- gain_one: bfloat16 [768], P('dp'), may hold values from 0.5 to 1.5
- shift_one: bfloat16 [768], P('dp'), may hold values from -3 to 3
- gain_two: bfloat16 [768], P('dp'), may hold values from 0.5 to 1.5
- shift_two: bfloat16 [768], P('dp'), may hold values from -3 to 3
Outputs:
- activations: bfloat16 [32, 1024, 768], P(('grp', 'dp'))
- input_grad: bfloat16 [32, 1024, 768], P(('grp', 'dp'))
- grad_w_qkv: float32 [768, 2304], P('dp')
- grad_w_out: float32 [768, 768], P('dp')
- grad_w_up: float32 [768, 3072], P('dp')
- grad_w_down: float32 [3072, 768], P('dp')
- grad_bias_q: float32 [768], P('dp')
- grad_bias_v: float32 [768], P('dp')
- grad_bias_out: float32 [768], P('dp')
- grad_bias_up: float32 [3072], P('dp')
- grad_bias_down: float32 [768], P('dp')
- grad_gain_one: float32 [768], P('dp')
- grad_shift_one: float32 [768], P('dp')
- grad_gain_two: float32 [768], P('dp')
- grad_shift_two: float32 [768], P('dp')
The draws below stay inside these ranges and needn't reach their ends.
Inputs may be any that keep to these rules, and one draw needn't show every extreme that they name: `lengths`: every sequence has at least 32 live tokens and at least one has 1024.
All inputs are finite; a program needn't handle non-finite values.
Results may differ from the reference program's by a relative error of at most 0.018.
Values may be sent and summed in bfloat16 or wider, within the bound.
A program may use at most 192 MiB of HBM per device.

```python
import math
import jax
import jax.numpy as jnp
from jax import lax

D = 768
HEADS = 12
FF = 3072
HEAD_DIM = 64
LENGTH = 1024
MIN_LEN = 32
TASKS = 16
SEQS = 32


def draw_lengths(key, part):
    key = jax.random.fold_in(key, 7)
    first, second = jax.random.split(key)
    values = jax.random.randint(first, (SEQS,), MIN_LEN, LENGTH + 1)
    where_full = jax.random.randint(second, (), 0, SEQS)
    return jnp.where(jnp.arange(SEQS) == where_full, LENGTH, values).astype(jnp.int32)


def place_ends(array, key, smallest, top_value):
    extent = array.shape
    spot = [jax.random.randint(jax.random.fold_in(key, axis), (), 0, extent[axis]) for axis in range(len(extent))]
    array = array.at[tuple(spot)].set(smallest)
    longest = extent.index(max(extent))
    spot[longest] = (spot[longest] + 1) % extent[longest]
    return array.at[tuple(spot)].set(top_value)


def levels(key, dims, cuts, least, top_value):
    def one(dim, parts):
        draws = jax.random.uniform(jax.random.fold_in(jax.random.fold_in(key, 6), dim), (parts,), jnp.float32, least / len(cuts), top_value / len(cuts))
        return jnp.repeat(jnp.exp(draws), dims[dim] // parts).reshape((-1,) + (1,) * (len(dims) - dim - 1))

    gain = one(*cuts[0])
    for cut in cuts[1:]:
        gain = gain * one(*cut)
    return gain


def gaussian(rng, dims, scale, limit, cuts=(), dtype=jnp.bfloat16):
    result = jax.random.normal(rng, dims, jnp.float32) * scale
    if len(cuts) > 0:
        result = levels(rng, dims, cuts, -0.22, 0.18) * result
    return jnp.clip(result, min=-limit, max=limit).astype(dtype)


def setup_inputs(seed: int = 0) -> dict:
    splits = jax.random.split(jax.random.key(seed), 19)
    tokens = gaussian(splits[0], (SEQS, LENGTH, D), 1.0, 6.0, ((0, 32),))
    grad_out = gaussian(splits[1], (SEQS, LENGTH, D), 1.0, 6.0, ((0, 32),))
    lengths = draw_lengths(jax.random.fold_in(splits[18], 71), 0)
    task_of = place_ends(jax.random.randint(splits[3], (SEQS,), 0, TASKS), jax.random.fold_in(splits[3], 1), 0, TASKS - 1).astype(jnp.int32)
    task_tokens = place_ends(jax.random.randint(splits[4], (TASKS,), 256, 4097), jax.random.fold_in(splits[4], 1), 256, 4096).astype(jnp.int32)
    w_qkv = gaussian(splits[5], (D, 3 * D), D ** -0.5, 0.21875, ((0, 8),))
    w_out = gaussian(splits[6], (D, D), (D // 64) ** -0.5, 1.75, ((0, 8),))
    w_up = gaussian(splits[7], (D, FF), D ** -0.5, 0.21875, ((0, 8),))
    w_down = gaussian(splits[8], (FF, D), FF ** -0.5, 0.109375, ((0, 8),))
    bias_q = gaussian(splits[9], (D,), 0.5, 3.0, ((0, 8),))
    bias_v = gaussian(splits[10], (D,), 0.5, 3.0, ((0, 8),))
    bias_out = gaussian(splits[11], (D,), 0.5, 3.0, ((0, 8),))
    bias_up = gaussian(splits[12], (FF,), 0.5, 3.0, ((0, 8),))
    bias_down = gaussian(splits[13], (D,), 0.5, 3.0, ((0, 8),))
    gain_one = jnp.clip(1.0 + 0.1 * jax.random.normal(splits[14], (D,), jnp.float32), 0.5, 1.5).astype(jnp.bfloat16)
    shift_one = gaussian(splits[15], (D,), 0.5, 3.0, ((0, 8),))
    gain_two = jnp.clip(1.0 + 0.1 * jax.random.normal(splits[16], (D,), jnp.float32), 0.5, 1.5).astype(jnp.bfloat16)
    shift_two = gaussian(splits[17], (D,), 0.5, 3.0, ((0, 8),))
    return {"tokens": tokens, "grad_out": grad_out, "lengths": lengths, "task_of": task_of, "task_tokens": task_tokens, "w_qkv": w_qkv, "w_out": w_out, "w_up": w_up, "w_down": w_down, "bias_q": bias_q, "bias_v": bias_v, "bias_out": bias_out, "bias_up": bias_up, "bias_down": bias_down, "gain_one": gain_one, "shift_one": shift_one, "gain_two": gain_two, "shift_two": shift_two}


@jax.custom_vjp
def low(v):
    return lax.optimization_barrier(v.astype(jnp.bfloat16)).astype(jnp.float32)

@jax.custom_vjp
def low_back(v):
    return v

def low_keep(v):
    return (low(v), None)

def low_pass(kept, grad):
    return (grad,)

def back_keep(v):
    return (v, None)

def back_low(kept, grad):
    return (low(grad),)
low.defvjp(low_keep, low_pass)
low_back.defvjp(back_keep, back_low)
EPS = 1e-05
UNIT = 1024.0
HIGH = lax.Precision.HIGHEST

def norm_rows(values):
    mean = lax.optimization_barrier(jnp.mean(values, axis=-1, keepdims=True))
    centered = values - mean
    return centered * lax.rsqrt(lax.optimization_barrier(jnp.mean(centered * centered, axis=-1, keepdims=True)) + EPS)

def hdot(left, right):
    return jnp.dot(left, right, precision=HIGH, preferred_element_type=jnp.float32)

def one_sequence(inputs, length_s, params):
    w_qkv, w_out, w_up, w_down, bias_q, bias_v, bias_out, bias_up, bias_down, gain_one, shift_one, gain_two, shift_two = params
    block = min(512, LENGTH)
    scale = HEAD_DIM ** (-0.5)
    a1 = low(norm_rows(inputs) * gain_one + shift_one)
    qkv = hdot(a1, w_qkv)
    query = low(low_back(qkv[:, :D] + bias_q)).reshape(LENGTH, HEADS, HEAD_DIM)
    key_all = low(low_back(qkv[:, D:2 * D])).reshape(LENGTH, HEADS, HEAD_DIM)
    value = low(low_back(qkv[:, 2 * D:] + bias_v)).reshape(LENGTH, HEADS, HEAD_DIM)
    columns = jnp.arange(LENGTH)

    def attend(item):
        q_block, start = item
        scores = jnp.einsum('qhd,khd->hqk', q_block, key_all, precision=HIGH) * scale
        scores = low_back(scores)
        rows = start + jnp.arange(block)
        allowed = (columns[None, :] <= rows[:, None]) & (columns[None, :] < length_s)
        scores = jnp.where(allowed[None], scores, -1e+30)
        probs = jnp.exp(scores - jax.nn.logsumexp(scores, axis=-1, keepdims=True))
        return jnp.einsum('hqk,khd->qhd', low(probs), value, precision=HIGH)
    starts = (jnp.arange(LENGTH // block) * block).astype(jnp.int32)
    blocks = query.reshape(LENGTH // block, block, HEADS, HEAD_DIM)
    att = lax.map(jax.checkpoint(attend), (blocks, starts)).reshape(LENGTH, D)
    att = low(low_back(att))
    x2 = inputs + low_back(hdot(att, w_out) + bias_out)
    a2 = low(norm_rows(x2) * gain_two + shift_two)
    hidden = low_back(hdot(a2, w_up) + bias_up)
    hidden = low(jax.nn.gelu(hidden, approximate=False))
    return x2 + low_back(hdot(hidden, w_down) + bias_down)

def reference(tokens, grad_out, lengths, task_of, task_tokens, w_qkv, w_out, w_up, w_down, bias_q, bias_v, bias_out, bias_up, bias_down, gain_one, shift_one, gain_two, shift_two):
    params = tuple((p.astype(jnp.float32) for p in (w_qkv, w_out, w_up, w_down, bias_q, bias_v, bias_out, bias_up, bias_down, gain_one, shift_one, gain_two, shift_two)))
    weight = UNIT / task_tokens[task_of].astype(jnp.float32)
    group = math.gcd(SEQS, max(1, 4096 // LENGTH))
    count = SEQS // group
    items = (tokens.reshape(count, group, LENGTH, D), grad_out.reshape(count, group, LENGTH, D), lengths.reshape(count, group), weight.reshape(count, group))

    def step(carry, item):
        span_in, span_grad, lens, weights = item
        inputs = span_in.astype(jnp.float32)
        valid = (jnp.arange(LENGTH)[None, :] < lens[:, None]).astype(jnp.float32)
        cotangent = span_grad.astype(jnp.float32) * (weights[:, None] * valid)[:, :, None]

        def forward(values, pars):
            return jax.vmap(lambda seq, length_s: one_sequence(seq, length_s, pars))(values, lens)
        outputs, pull = jax.vjp(forward, inputs, params)
        grad_in, grad_pars = pull(cotangent)
        carry = tuple((c + g for c, g in zip(carry, grad_pars)))
        return (carry, (outputs.astype(jnp.bfloat16), grad_in.astype(jnp.bfloat16)))
    start_sums = tuple((jnp.zeros(p.shape, jnp.float32) for p in params))
    totals, (outputs, grads_in) = lax.scan(step, start_sums, items)
    outputs = outputs.reshape(SEQS, LENGTH, D)
    grads_in = grads_in.reshape(SEQS, LENGTH, D)
    return (outputs, grads_in, totals[0], totals[1], totals[2], totals[3], totals[4], totals[5], totals[6], totals[7], totals[8], totals[9], totals[10], totals[11], totals[12])
```

```python
import functools
import math

import jax
import jax.numpy as jnp
from jax import lax
from jax.experimental import pallas as pl
from jax.experimental.pallas import tpu as pltpu
from jax.sharding import PartitionSpec as P

F32 = jnp.float32
BF16 = jnp.bfloat16
EPS = 1e-05
UNIT = 1024.0
HEAD = 64
BLOCK = 256
TILE = 512
BQ, BV, BO, BD, G1, S1, G2, S2, UP = range(9)
VEC_ROWS = 16


def dot(left, right, left_dim, right_dim):
    return lax.dot_general(
        left, right, (((left_dim,), (right_dim,)), ((), ())), preferred_element_type=F32
    )


def nn(left, right):
    return dot(left, right, 1, 0)


def nt(left, right):
    return dot(left, right, 1, 1)


def tn(left, right):
    return dot(left, right, 0, 0)


def norm_rows(values):
    mean = jnp.mean(values, axis=-1, keepdims=True)
    centered = values - mean
    rstd = lax.rsqrt(jnp.mean(centered * centered, axis=-1, keepdims=True) + EPS)
    return centered * rstd, rstd


def norm_back(grad_norm, normed, rstd):
    mean_one = jnp.mean(grad_norm, axis=-1, keepdims=True)
    mean_two = jnp.mean(grad_norm * normed, axis=-1, keepdims=True)
    return rstd * (grad_norm - mean_one - normed * mean_two)


def column_sum(values):
    return jnp.sum(values, axis=0, keepdims=True)


def rows_at(index, size=BLOCK):
    return pl.ds(pl.multiple_of(index * size, size), size)


def norm_one_phase(x, vecs, a1):
    gain, shift = vecs[G1 : G1 + 1, :], vecs[S1 : S1 + 1, :]

    def step(i, _):
        at = rows_at(i)
        normed, _ = norm_rows(x[at, :].astype(F32))
        a1[at, :] = (normed * gain + shift).astype(BF16)
        return 0

    lax.fori_loop(0, x.shape[0] // BLOCK, step, 0)


def qkv_phase(j, a1, wqkv, vecs, k, v, q_t, k_t, v_t):
    at = rows_at(j)
    values = nn(a1[...], wqkv[j])
    bias_q, bias_v = vecs[BQ : BQ + 1, at], vecs[BV : BV + 1, at]
    query = (values[:, :BLOCK] + bias_q).astype(BF16) * (HEAD**-0.5)
    key_all = values[:, BLOCK : 2 * BLOCK].astype(BF16)
    value = (values[:, 2 * BLOCK :] + bias_v).astype(BF16)
    k[:, at] = key_all
    v[:, at] = value
    q_t[at, :] = query.T
    k_t[at, :] = key_all.T
    v_t[at, :] = value.T


def padded(rows, side):
    zeros = jnp.zeros_like(rows)
    return jnp.concatenate([rows, zeros] if side == 0 else [zeros, rows], axis=0)


def attend_pair(p, length_s, k, q_t, v_t, o_t, o, lse):
    length = k.shape[0]
    lanes = rows_at(p, 2 * HEAD)
    for i in range(length // BLOCK):
        cols = slice(i * BLOCK, (i + 1) * BLOCK)
        seen = (i + 1) * BLOCK
        queries = i * BLOCK + lax.broadcasted_iota(jnp.int32, (1, BLOCK), 1)
        limit = jnp.minimum(queries + 1, length_s)
        key_index = lax.broadcasted_iota(jnp.int32, (seen, BLOCK), 0)
        allowed = key_index < limit
        halves = []
        for side in range(2):
            head = 2 * p + side
            at = rows_at(head, HEAD)
            scores = nn(k[:seen, lanes], padded(q_t[at, cols], side))
            scores = jnp.where(allowed, scores, -1e30)
            top = jnp.max(scores, axis=0, keepdims=True)
            weights = jnp.exp(scores - top)
            total = jnp.sum(weights, axis=0, keepdims=True)
            lse[head, :, cols] = jnp.where(queries < length_s, top + jnp.log(total), 1e30)
            result = nn(v_t[at, :seen], weights.astype(BF16)) * (1.0 / total)
            halves.append(result.astype(BF16))
        both = jnp.concatenate(halves, axis=0)
        o_t[lanes, cols] = both
        o[cols, lanes] = both.T


def attend_back_pair(p, k, v, q_t, k_t, g_o_t, lse, delta, dk_t, dv_t, dqkv, gvec):
    length = k.shape[0]
    count = length // BLOCK
    lanes = rows_at(p, 2 * HEAD)
    dq_sides = []
    for side in range(2):
        head = 2 * p + side
        at = rows_at(head, HEAD)
        here = slice(side * HEAD, (side + 1) * HEAD)
        dq_parts = []
        for i in reversed(range(count)):
            cols = slice(i * BLOCK, (i + 1) * BLOCK)
            seen = (i + 1) * BLOCK
            q_cols, g_cols = q_t[at, cols], g_o_t[at, cols]
            scores = nn(k[:seen, lanes], padded(q_cols, side))
            key_index = lax.broadcasted_iota(jnp.int32, (BLOCK, BLOCK), 0)
            query_index = lax.broadcasted_iota(jnp.int32, (BLOCK, BLOCK), 1)
            diagonal = jnp.where(key_index <= query_index, scores[seen - BLOCK :], -1e30)
            if i > 0:
                scores = jnp.concatenate([scores[: seen - BLOCK], diagonal], axis=0)
            else:
                scores = diagonal
            probs = jnp.exp(scores - lse[head, :, cols])
            grad_probs = nn(v[:seen, lanes], padded(g_cols, side))
            grad_scores = (probs * (grad_probs - delta[head, :, cols])).astype(BF16)
            part_v = nt(g_cols, probs.astype(BF16))
            part_k = nt(q_cols, grad_scores)
            if i == count - 1:
                dv_t[here, :] = part_v
                dk_t[here, :] = part_k
            else:
                dv_t[here, :seen] += part_v
                dk_t[here, :seen] += part_k
            dq_parts.append(nn(k_t[at, :seen], grad_scores) * (HEAD**-0.5))
        dq_sides.append(jnp.concatenate(dq_parts[::-1], axis=1).astype(BF16))
    dq = jnp.concatenate(dq_sides, axis=0).T
    dk = dk_t[...].astype(BF16).T
    dv = dv_t[...].astype(BF16).T
    base = lax.rem(p, 2) * (2 * HEAD)
    for part, value in enumerate((dq, dk, dv)):
        place = pl.ds(pl.multiple_of(base + part * BLOCK, 2 * HEAD), 2 * HEAD)
        dqkv[:, place] = value
    gvec[BQ : BQ + 1, lanes] = column_sum(dq.astype(F32))
    gvec[BV : BV + 1, lanes] = column_sum(dv.astype(F32))


def norm_two_phase(x, o, wout, vecs, x2, a2, out_acc):
    bias, down = vecs[BO : BO + 1, :], vecs[BD : BD + 1, :]
    gain, shift = vecs[G2 : G2 + 1, :], vecs[S2 : S2 + 1, :]

    def step(i, _):
        at = rows_at(i)
        value = x[at, :].astype(F32) + nn(o[at, :], wout[...]) + bias
        x2[at, :] = value
        out_acc[at, :] = value + down
        normed, _ = norm_rows(value)
        a2[at, :] = (normed * gain + shift).astype(BF16)
        return 0

    lax.fori_loop(0, x.shape[0] // BLOCK, step, 0)


def cotangent_rows(i, grad_out, length_s, weight_s):
    at = rows_at(i)
    index = i * BLOCK + lax.broadcasted_iota(jnp.int32, (BLOCK, 1), 0)
    scale = jnp.where(index < length_s, weight_s, 0.0)
    return grad_out[at, :].astype(F32) * scale


def branch_phase(grad_out, length_s, weight_s, g_f, gvec):
    def step(i, total):
        rounded = cotangent_rows(i, grad_out, length_s, weight_s).astype(BF16)
        g_f[rows_at(i), :] = rounded
        return total + column_sum(rounded.astype(F32))

    width = grad_out.shape[1]
    total = lax.fori_loop(0, grad_out.shape[0] // BLOCK, step, jnp.zeros((1, width), F32))
    gvec[BD : BD + 1, :] = total


def hidden_tile(t, a2, g_f, wup, wdn, vecs, out_acc, da2, hr, gu, gvec):
    length = a2.shape[0]
    up, down = wup[t], wdn[t]
    bias = vecs[pl.ds(UP + t, 1), :TILE]
    total = jnp.zeros((1, TILE), F32)
    for m in range(length // BLOCK):
        at = slice(m * BLOCK, (m + 1) * BLOCK)
        u = nn(a2[at, :], up) + bias
        dh = nt(g_f[at, :], down)
        cdf = 0.5 + 0.5 * lax.erf(u * (1.0 / math.sqrt(2.0)))
        slope = cdf + u * (jnp.exp(-0.5 * u * u) * (1.0 / math.sqrt(2.0 * math.pi)))
        hidden = (u * cdf).astype(BF16)
        g_u = (dh * slope).astype(BF16)
        hr[at, :] = hidden
        gu[at, :] = g_u
        total = total + column_sum(g_u.astype(F32))
        out_acc[at, :] += nn(hidden, down)
        da2[at, :] += nt(g_u, up)
    gvec[pl.ds(UP + t, 1), :TILE] = total


def norm_two_back(grad_out, length_s, weight_s, x2, da2, vecs, g_a, gvec, out_acc, act):
    gain = vecs[G2 : G2 + 1, :]
    width = x2.shape[1]

    def step(i, carry):
        at = rows_at(i)
        act[at, :] = out_acc[at, :].astype(BF16)
        normed, rstd = norm_rows(x2[at, :])
        grad = da2[at, :]
        dx2 = cotangent_rows(i, grad_out, length_s, weight_s) + norm_back(grad * gain, normed, rstd)
        da2[at, :] = dx2
        rounded = dx2.astype(BF16)
        g_a[at, :] = rounded
        return (
            carry[0] + column_sum(grad * normed),
            carry[1] + column_sum(grad),
            carry[2] + column_sum(rounded.astype(F32)),
        )

    zero = jnp.zeros((1, width), F32)
    sums = lax.fori_loop(0, x2.shape[0] // BLOCK, step, (zero, zero, zero))
    gvec[G2 : G2 + 1, :], gvec[S2 : S2 + 1, :], gvec[BO : BO + 1, :] = sums


def attended_back(wout, g_a, o_t, g_o_t, delta):
    for i in range(g_a.shape[0] // BLOCK):
        cols = slice(i * BLOCK, (i + 1) * BLOCK)
        grad = nt(wout[...], g_a[cols, :]).astype(BF16)
        g_o_t[:, cols] = grad
        product = grad.astype(F32) * o_t[:, cols].astype(F32)
        for head in range(wout.shape[0] // HEAD):
            delta[head, :, cols] = column_sum(product[head * HEAD : (head + 1) * HEAD])


def norm_one_back(x, dx2, da1, vecs, gvec, input_grad):
    gain = vecs[G1 : G1 + 1, :]
    width = x.shape[1]

    def step(i, carry):
        at = rows_at(i)
        normed, rstd = norm_rows(x[at, :].astype(F32))
        grad = da1[at, :]
        result = dx2[at, :] + norm_back(grad * gain, normed, rstd)
        input_grad[at, :] = result.astype(BF16)
        return (carry[0] + column_sum(grad * normed), carry[1] + column_sum(grad))

    zero = jnp.zeros((1, width), F32)
    sums = lax.fori_loop(0, x.shape[0] // BLOCK, step, (zero, zero))
    gvec[G1 : G1 + 1, :], gvec[S1 : S1 + 1, :] = sums


def task_weight(task_of, task_tokens):
    return UNIT / task_tokens[task_of[0]].astype(F32)


def layer_body(comm, lengths, task_of, task_tokens, x, grad_out, act, input_grad, w, s):
    length_s = lengths[0]
    weight_s = task_weight(task_of, task_tokens)
    wqkv, wout, wup, wdn, vecs = w
    s.gvec[...] = jnp.zeros_like(s.gvec)
    s.da2[...] = jnp.zeros_like(s.da2)
    comm.begin()
    norm_one_phase(x, vecs, s.a1)
    branch_phase(grad_out, length_s, weight_s, s.g_f, s.gvec)

    def forward(j, _):
        comm.need_qkv(j)
        qkv_phase(j, s.a1, wqkv, vecs, s.k, s.v, s.q_t, s.k_t, s.v_t)

        def pair(p, _):
            attend_pair(2 * j + p, length_s, s.k, s.q_t, s.v_t, s.o_t, s.o, s.lse)
            return 0

        return lax.fori_loop(0, 2, pair, 0)

    lax.fori_loop(0, wqkv.shape[0], forward, 0)
    comm.need_out()
    norm_two_phase(x, s.o, wout, vecs, s.x2, s.a2, s.out_acc)

    def hidden(t, _):
        comm.need_hidden(t)
        hidden_tile(t, s.a2, s.g_f, wup, wdn, vecs, s.out_acc, s.da2, s.hr, s.gu, s.gvec)
        comm.give_up(t, lambda: tn(s.a2[...], s.gu[...]).astype(BF16))
        comm.give_down(t, lambda: tn(s.hr[...], s.g_f[...]).astype(BF16))
        return 0

    lax.fori_loop(0, wup.shape[0], hidden, 0)
    norm_two_back(
        grad_out, length_s, weight_s, s.x2, s.da2, vecs, s.a2, s.gvec, s.out_acc, s.g_f
    )
    act_copy = pltpu.make_async_copy(s.g_f, act, s.local.at[0])
    act_copy.start()
    comm.give_out(lambda: tn(s.o[...], s.a2[...]).astype(BF16))
    attended_back(wout, s.a2, s.o_t, s.g_o_t, s.delta)
    da1 = s.out_acc
    da1[...] = jnp.zeros_like(da1)

    def backward(j, _):
        def pair(p, _):
            attend_back_pair(
                2 * j + p, s.k, s.v, s.q_t, s.k_t, s.g_o_t, s.lse, s.delta,
                s.dk_t, s.dv_t, s.dqkv, s.gvec,
            )
            return 0

        lax.fori_loop(0, 2, pair, 0)
        comm.give_qkv(j, lambda: tn(s.a1[...], s.dqkv[...]).astype(BF16))
        for m in range(x.shape[0] // BLOCK):
            at = slice(m * BLOCK, (m + 1) * BLOCK)
            da1[at, :] += nt(s.dqkv[at, :], wqkv[j])
        return 0

    lax.fori_loop(0, wqkv.shape[0], backward, 0)
    norm_one_back(x, s.da2, da1, vecs, s.gvec, s.a1)
    grad_copy = pltpu.make_async_copy(s.a1, input_grad, s.local.at[1])
    grad_copy.start()
    comm.end()
    act_copy.wait()
    grad_copy.wait()


class Named:
    def __init__(self, names, refs):
        for name, ref in zip(names, refs):
            setattr(self, name, ref)


def layer_scratch(length, width):
    heads = width // HEAD
    wide, tall = (length, width), (width, length)
    return {
        "a1": pltpu.VMEM(wide, BF16),
        "k": pltpu.VMEM(wide, BF16),
        "v": pltpu.VMEM(wide, BF16),
        "q_t": pltpu.VMEM(tall, BF16),
        "k_t": pltpu.VMEM(tall, BF16),
        "v_t": pltpu.VMEM(tall, BF16),
        "o_t": pltpu.VMEM(tall, BF16),
        "o": pltpu.VMEM(wide, BF16),
        "g_o_t": pltpu.VMEM(tall, BF16),
        "lse": pltpu.VMEM((heads, 1, length), F32),
        "delta": pltpu.VMEM((heads, 1, length), F32),
        "x2": pltpu.VMEM(wide, F32),
        "a2": pltpu.VMEM(wide, BF16),
        "out_acc": pltpu.VMEM(wide, F32),
        "da2": pltpu.VMEM(wide, F32),
        "g_f": pltpu.VMEM(wide, BF16),
        "hr": pltpu.VMEM((length, TILE), BF16),
        "gu": pltpu.VMEM((length, TILE), BF16),
        "dk_t": pltpu.VMEM((2 * HEAD, length), F32),
        "dv_t": pltpu.VMEM((2 * HEAD, length), F32),
        "dqkv": pltpu.VMEM((length, 3 * BLOCK), BF16),
        "gvec": pltpu.VMEM((VEC_ROWS, width), F32),
        "local": pltpu.SemaphoreType.DMA((2,)),
    }


class Plain:
    def __init__(self, outs, stage, sem):
        self.outs, self.stage, self.sem = outs, stage, sem

    def begin(self):
        pass

    need_qkv = need_hidden = need_out = lambda self, *args: None

    def put(self, stage, place, make):
        stage[...] = make()
        copy = pltpu.make_async_copy(stage, place, self.sem)
        copy.start()
        copy.wait()

    def give_up(self, t, make):
        self.put(self.stage[1], self.outs[2].at[t], make)

    def give_down(self, t, make):
        self.put(self.stage[2], self.outs[3].at[t], make)

    def give_out(self, make):
        self.put(self.stage[0], self.outs[1], make)

    def give_qkv(self, j, make):
        self.put(self.stage[0], self.outs[0].at[j], make)

    def end(self):
        pass


def plain_layer(lengths, task_of, task_tokens, x, grad_out, wqkv, wout, wup, wdn, vecs):
    length, width = x.shape
    scratch = layer_scratch(length, width)
    names = tuple(scratch)

    def kernel(*refs):
        (lens, of, tokens, x, g, wqkv, wout, wup, wdn, vecs) = refs[:10]
        act, input_grad, gqkv, gout, gup, gdn, gvec = refs[10:17]
        s = Named(names, refs[17 : 17 + len(names)])
        rest = refs[17 + len(names) :]
        comm = Plain((gqkv, gout, gup, gdn), rest[:3], rest[3])
        layer_body(comm, lens, of, tokens, x, g, act, input_grad, (wqkv, wout, wup, wdn, vecs), s)
        gvec[...] = s.gvec[...]

    smem = pl.BlockSpec(memory_space=pltpu.SMEM)
    vmem = pl.BlockSpec(memory_space=pltpu.VMEM)
    hbm = pl.BlockSpec(memory_space=pl.ANY)
    like = lambda a: jax.ShapeDtypeStruct(a.shape, BF16)
    return pl.pallas_call(
        kernel,
        out_shape=(
            like(x), like(x), like(wqkv), like(wout), like(wup), like(wdn),
            jax.ShapeDtypeStruct((VEC_ROWS, width), F32),
        ),
        in_specs=[smem] * 3 + [vmem] * 7,
        out_specs=(hbm,) * 6 + (vmem,),
        scratch_shapes=list(scratch.values())
        + [
            pltpu.VMEM((width, width), BF16),
            pltpu.VMEM((width, TILE), BF16),
            pltpu.VMEM((TILE, width), BF16),
            pltpu.SemaphoreType.DMA,
        ],
        compiler_params=pltpu.CompilerParams(vmem_limit_bytes=62 * 2**20),
        name="layer",
    )(lengths, task_of, task_tokens, x, grad_out, wqkv, wout, wup, wdn, vecs)


def pack_vectors(bias_q, bias_v, bias_out, bias_up, bias_down, gain_one, shift_one, gain_two, shift_two):
    width = bias_q.shape[0]
    rows = jnp.stack([bias_q, bias_v, bias_out, bias_down, gain_one, shift_one, gain_two, shift_two])
    tiles = jnp.pad(bias_up.reshape(-1, TILE), ((0, 0), (0, width - TILE)))
    rest = jnp.zeros((VEC_ROWS - rows.shape[0] - tiles.shape[0], width), BF16)
    return jnp.concatenate([rows, tiles, rest]).astype(F32)


def plain_body(
    tokens, grad_out, lengths, task_of, task_tokens, w_qkv, w_out, w_up, w_down,
    bias_q, bias_v, bias_out, bias_up, bias_down, gain_one, shift_one, gain_two, shift_two,
):
    gather = lambda a: lax.all_gather(a, "dp", axis=0, tiled=True)
    width = tokens.shape[2]
    chunks, tiles = width // BLOCK, w_up.shape[1] // TILE
    wqkv = gather(w_qkv).reshape(width, 3, chunks, BLOCK).transpose(2, 0, 1, 3)
    wqkv = wqkv.reshape(chunks, width, 3 * BLOCK)
    wup = gather(w_up).reshape(width, tiles, TILE).transpose(1, 0, 2)
    wdn = gather(w_down).reshape(tiles, TILE, width)
    vecs = pack_vectors(
        *(gather(a) for a in (bias_q, bias_v, bias_out, bias_up, bias_down, gain_one, shift_one, gain_two, shift_two))
    )
    act, input_grad, gqkv, gout, gup, gdn, gvec = plain_layer(
        lengths, task_of, task_tokens, tokens[0], grad_out[0], wqkv, gather(w_out), wup, wdn, vecs
    )
    gqkv = gqkv.reshape(chunks, width, 3, BLOCK).transpose(1, 2, 0, 3).reshape(width, 3 * width)
    gup = gup.transpose(1, 0, 2).reshape(width, -1)
    gdn = gdn.reshape(-1, width)
    vectors = [gvec[BQ], gvec[BV], gvec[BO], gvec[UP : UP + tiles, :TILE].reshape(-1), gvec[BD]]
    vectors += [gvec[G1], gvec[S1], gvec[G2], gvec[S2]]
    grads = [gqkv, gout, gup, gdn] + [a.astype(BF16) for a in vectors]
    shares = lax.psum_scatter(grads, "dp", scatter_dimension=0, tiled=True)
    summed = jax.tree.map(lambda a: a.astype(F32), lax.psum(shares, "grp"))
    return (act[None], input_grad[None], *summed)


def solution(mesh):
    rows = P(("grp", "dp"), None, None)
    each = P(("grp", "dp"))
    matrix, vector = P("dp", None), P("dp")
    in_specs = (rows, rows, each, each, P()) + (matrix,) * 4 + (vector,) * 9
    out_specs = (rows, rows) + (matrix,) * 4 + (vector,) * 9
    body = plain_body
    return jax.shard_map(body, mesh=mesh, in_specs=in_specs, out_specs=out_specs, check_vma=False)
```

```python
import functools
import math

import jax
import jax.numpy as jnp
from jax import lax
from jax.experimental import pallas as pl
from jax.experimental.pallas import tpu as pltpu
from jax.sharding import PartitionSpec as P

F32 = jnp.float32
BF16 = jnp.bfloat16
EPS = 1e-05
UNIT = 1024.0
HEAD = 64
BLOCK = 256
TILE = 512
BQ, BV, BO, BD, G1, S1, G2, S2, UP = range(9)
VEC_ROWS = 16


def dot(left, right, left_dim, right_dim):
    return lax.dot_general(
        left, right, (((left_dim,), (right_dim,)), ((), ())), preferred_element_type=F32
    )


def nn(left, right):
    return dot(left, right, 1, 0)


def nt(left, right):
    return dot(left, right, 1, 1)


def tn(left, right):
    return dot(left, right, 0, 0)


def norm_rows(values):
    mean = jnp.mean(values, axis=-1, keepdims=True)
    centered = values - mean
    rstd = lax.rsqrt(jnp.mean(centered * centered, axis=-1, keepdims=True) + EPS)
    return centered * rstd, rstd


def norm_back(grad_norm, normed, rstd):
    mean_one = jnp.mean(grad_norm, axis=-1, keepdims=True)
    mean_two = jnp.mean(grad_norm * normed, axis=-1, keepdims=True)
    return rstd * (grad_norm - mean_one - normed * mean_two)


def column_sum(values):
    return jnp.sum(values, axis=0, keepdims=True)


def rows_at(index, size=BLOCK):
    return pl.ds(pl.multiple_of(index * size, size), size)


def norm_one_phase(x, vecs, a1, x2):
    gain, shift = vecs[G1 : G1 + 1, :], vecs[S1 : S1 + 1, :]

    def step(i, _):
        at = rows_at(i)
        value = x[at, :].astype(F32)
        x2[at, :] = value
        normed, _ = norm_rows(value)
        a1[at, :] = (normed * gain + shift).astype(BF16)
        return 0

    lax.fori_loop(0, x.shape[0] // BLOCK, step, 0)


def qkv_phase(j, a1, wqkv, vecs, k, v, q_t, k_t, v_t):
    at = rows_at(j)
    values = nn(a1[...], wqkv[j])
    bias_q, bias_v = vecs[BQ : BQ + 1, at], vecs[BV : BV + 1, at]
    query = (values[:, :BLOCK] + bias_q).astype(BF16) * (HEAD**-0.5)
    key_all = values[:, BLOCK : 2 * BLOCK].astype(BF16)
    value = (values[:, 2 * BLOCK :] + bias_v).astype(BF16)
    k[:, at] = key_all
    v[:, at] = value
    q_t[at, :] = query.T
    k_t[at, :] = key_all.T
    v_t[at, :] = value.T


def padded(rows, side):
    zeros = jnp.zeros_like(rows)
    return jnp.concatenate([rows, zeros] if side == 0 else [zeros, rows], axis=0)


def attend_pair(p, length_s, k, q_t, v_t, o_t, lse):
    length = k.shape[0]
    lanes = rows_at(p, 2 * HEAD)
    for i in range(length // BLOCK):
        cols = slice(i * BLOCK, (i + 1) * BLOCK)
        seen = (i + 1) * BLOCK
        queries = i * BLOCK + lax.broadcasted_iota(jnp.int32, (1, BLOCK), 1)
        limit = jnp.minimum(queries + 1, length_s)
        key_index = lax.broadcasted_iota(jnp.int32, (seen, BLOCK), 0)
        allowed = key_index < limit
        halves = []
        for side in range(2):
            head = 2 * p + side
            at = rows_at(head, HEAD)
            scores = nn(k[:seen, lanes], padded(q_t[at, cols], side))
            scores = jnp.where(allowed, scores, -1e30)
            top = jnp.max(scores, axis=0, keepdims=True)
            weights = jnp.exp(scores - top)
            total = jnp.sum(weights, axis=0, keepdims=True)
            lse[head, :, cols] = jnp.where(queries < length_s, top + jnp.log(total), 1e30)
            result = nn(v_t[at, :seen], weights.astype(BF16)) * (1.0 / total)
            halves.append(result.astype(BF16))
        o_t[lanes, cols] = jnp.concatenate(halves, axis=0)


def attend_back_pair(p, k, v, q_t, k_t, g_o_t, lse, delta, dk_t, dv_t, dqkv, gvec):
    length = k.shape[0]
    count = length // BLOCK
    lanes = rows_at(p, 2 * HEAD)
    dq_sides = []
    for side in range(2):
        head = 2 * p + side
        at = rows_at(head, HEAD)
        here = slice(side * HEAD, (side + 1) * HEAD)
        dq_parts = []
        for i in reversed(range(count)):
            cols = slice(i * BLOCK, (i + 1) * BLOCK)
            seen = (i + 1) * BLOCK
            q_cols, g_cols = q_t[at, cols], g_o_t[at, cols]
            scores = nn(k[:seen, lanes], padded(q_cols, side))
            key_index = lax.broadcasted_iota(jnp.int32, (BLOCK, BLOCK), 0)
            query_index = lax.broadcasted_iota(jnp.int32, (BLOCK, BLOCK), 1)
            diagonal = jnp.where(key_index <= query_index, scores[seen - BLOCK :], -1e30)
            if i > 0:
                scores = jnp.concatenate([scores[: seen - BLOCK], diagonal], axis=0)
            else:
                scores = diagonal
            probs = jnp.exp(scores - lse[head, :, cols])
            grad_probs = nn(v[:seen, lanes], padded(g_cols, side))
            grad_scores = (probs * (grad_probs - delta[head, :, cols])).astype(BF16)
            part_v = nt(g_cols, probs.astype(BF16))
            part_k = nt(q_cols, grad_scores)
            if i == count - 1:
                dv_t[here, :] = part_v
                dk_t[here, :] = part_k
            else:
                dv_t[here, :seen] += part_v
                dk_t[here, :seen] += part_k
            dq_parts.append(nn(k_t[at, :seen], grad_scores) * (HEAD**-0.5))
        dq_sides.append(jnp.concatenate(dq_parts[::-1], axis=1).astype(BF16))
    dq = jnp.concatenate(dq_sides, axis=0).T
    dk = dk_t[...].astype(BF16).T
    dv = dv_t[...].astype(BF16).T
    base = lax.rem(p, 2) * (2 * HEAD)
    for part, value in enumerate((dq, dk, dv)):
        place = pl.ds(pl.multiple_of(base + part * BLOCK, 2 * HEAD), 2 * HEAD)
        dqkv[:, place] = value
    gvec[BQ : BQ + 1, lanes] = column_sum(dq.astype(F32))
    gvec[BV : BV + 1, lanes] = column_sum(dv.astype(F32))


def norm_two_phase(o_t, wout, vecs, x2, a2, out_acc):
    bias, down = vecs[BO : BO + 1, :], vecs[BD : BD + 1, :]
    gain, shift = vecs[G2 : G2 + 1, :], vecs[S2 : S2 + 1, :]

    for i in range(x2.shape[0] // BLOCK):
        at = slice(i * BLOCK, (i + 1) * BLOCK)
        value = x2[at, :] + tn(o_t[:, at], wout[...]) + bias
        x2[at, :] = value
        out_acc[at, :] = value + down
        normed, _ = norm_rows(value)
        a2[at, :] = (normed * gain + shift).astype(BF16)


def cotangent_rows(i, grad_out, length_s, weight_s):
    at = rows_at(i)
    index = i * BLOCK + lax.broadcasted_iota(jnp.int32, (BLOCK, 1), 0)
    scale = jnp.where(index < length_s, weight_s, 0.0)
    return grad_out[at, :].astype(F32) * scale


def branch_phase(grad_out, length_s, weight_s, g_f, gvec):
    def step(i, total):
        rounded = cotangent_rows(i, grad_out, length_s, weight_s).astype(BF16)
        g_f[rows_at(i), :] = rounded
        return total + column_sum(rounded.astype(F32))

    width = grad_out.shape[1]
    total = lax.fori_loop(0, grad_out.shape[0] // BLOCK, step, jnp.zeros((1, width), F32))
    gvec[BD : BD + 1, :] = total


def hidden_tile(t, a2, g_f, wup, wdn, vecs, out_acc, da2, hr, gu, gvec):
    length = a2.shape[0]
    up, down = wup[t], wdn[t]
    bias = vecs[pl.ds(UP + t, 1), :TILE]
    total = jnp.zeros((1, TILE), F32)
    for m in range(length // BLOCK):
        at = slice(m * BLOCK, (m + 1) * BLOCK)
        u = nn(a2[at, :], up) + bias
        dh = nt(g_f[at, :], down)
        cdf = 0.5 + 0.5 * lax.erf(u * (1.0 / math.sqrt(2.0)))
        slope = cdf + u * (jnp.exp(-0.5 * u * u) * (1.0 / math.sqrt(2.0 * math.pi)))
        hidden = (u * cdf).astype(BF16)
        g_u = (dh * slope).astype(BF16)
        hr[at, :] = hidden
        gu[at, :] = g_u
        total = total + column_sum(g_u.astype(F32))
        out_acc[at, :] += nn(hidden, down)
        da2[at, :] += nt(g_u, up)
    gvec[pl.ds(UP + t, 1), :TILE] = total


def norm_two_back(grad_out, length_s, weight_s, x2, da2, vecs, g_a, gvec, out_acc, act):
    gain = vecs[G2 : G2 + 1, :]
    width = x2.shape[1]

    def step(i, carry):
        at = rows_at(i)
        act[at, :] = out_acc[at, :].astype(BF16)
        normed, rstd = norm_rows(x2[at, :])
        grad = da2[at, :]
        dx2 = cotangent_rows(i, grad_out, length_s, weight_s) + norm_back(grad * gain, normed, rstd)
        da2[at, :] = dx2
        rounded = dx2.astype(BF16)
        g_a[at, :] = rounded
        return (
            carry[0] + column_sum(grad * normed),
            carry[1] + column_sum(grad),
            carry[2] + column_sum(rounded.astype(F32)),
        )

    zero = jnp.zeros((1, width), F32)
    sums = lax.fori_loop(0, x2.shape[0] // BLOCK, step, (zero, zero, zero))
    gvec[G2 : G2 + 1, :], gvec[S2 : S2 + 1, :], gvec[BO : BO + 1, :] = sums


def attended_back(wout, g_a, o_t, g_o_t, delta):
    for i in range(g_a.shape[0] // BLOCK):
        cols = slice(i * BLOCK, (i + 1) * BLOCK)
        grad = nt(wout[...], g_a[cols, :]).astype(BF16)
        g_o_t[:, cols] = grad
        product = grad.astype(F32) * o_t[:, cols].astype(F32)
        for head in range(wout.shape[0] // HEAD):
            delta[head, :, cols] = column_sum(product[head * HEAD : (head + 1) * HEAD])


def norm_one_back(x, dx2, da1, vecs, gvec, input_grad):
    gain = vecs[G1 : G1 + 1, :]
    width = x.shape[1]

    def step(i, carry):
        at = rows_at(i)
        normed, rstd = norm_rows(x[at, :].astype(F32))
        grad = da1[at, :]
        result = dx2[at, :] + norm_back(grad * gain, normed, rstd)
        input_grad[at, :] = result.astype(BF16)
        return (carry[0] + column_sum(grad * normed), carry[1] + column_sum(grad))

    zero = jnp.zeros((1, width), F32)
    sums = lax.fori_loop(0, x.shape[0] // BLOCK, step, (zero, zero))
    gvec[G1 : G1 + 1, :], gvec[S1 : S1 + 1, :] = sums


def task_weight(task_of, task_tokens):
    return UNIT / task_tokens[task_of[0]].astype(F32)


def layer_body(comm, lengths, task_of, task_tokens, x, grad_out, act, input_grad, w, s):
    length_s = lengths[0]
    weight_s = task_weight(task_of, task_tokens)
    wqkv, wout, wup, wdn, vecs = w
    s.gvec[...] = jnp.zeros_like(s.gvec)
    s.da2[...] = jnp.zeros_like(s.da2)
    comm.begin()
    norm_one_phase(x, vecs, s.a1, s.x2)
    branch_phase(grad_out, length_s, weight_s, s.g_f, s.gvec)

    def forward(j, _):
        comm.need_qkv(j)
        qkv_phase(j, s.a1, wqkv, vecs, s.k, s.v, s.q_t, s.k_t, s.v_t)

        def pair(p, _):
            attend_pair(2 * j + p, length_s, s.k, s.q_t, s.v_t, s.o_t, s.lse)
            return 0

        return lax.fori_loop(0, 2, pair, 0)

    lax.fori_loop(0, wqkv.shape[0], forward, 0)
    comm.need_out()
    norm_two_phase(s.o_t, wout, vecs, s.x2, s.a2, s.out_acc)

    hr, gu, dqkv = s.work.at[:, :TILE], s.work.at[:, TILE:], s.work.at[:, : 3 * BLOCK]
    g_o_t = s.v_t

    def hidden(t, _):
        comm.need_hidden(t)
        hidden_tile(t, s.a2, s.g_f, wup, wdn, vecs, s.out_acc, s.da2, hr, gu, s.gvec)
        comm.give_up(t, lambda: tn(s.a2[...], gu[...]).astype(BF16))
        comm.give_down(t, lambda: tn(hr[...], s.g_f[...]).astype(BF16))
        return 0

    lax.fori_loop(0, wup.shape[0], hidden, 0)
    norm_two_back(
        grad_out, length_s, weight_s, s.x2, s.da2, vecs, s.a2, s.gvec, s.out_acc, s.g_f
    )
    act_copy = pltpu.make_async_copy(s.g_f, act, s.local.at[0])
    act_copy.start()
    comm.give_out(lambda: nn(s.o_t[...], s.a2[...]).astype(BF16))
    attended_back(wout, s.a2, s.o_t, g_o_t, s.delta)
    da1 = s.out_acc
    da1[...] = jnp.zeros_like(da1)

    def backward(j, _):
        def pair(p, _):
            attend_back_pair(
                2 * j + p, s.k, s.v, s.q_t, s.k_t, g_o_t, s.lse, s.delta,
                s.dk_t, s.dv_t, dqkv, s.gvec,
            )
            return 0

        lax.fori_loop(0, 2, pair, 0)
        comm.give_qkv(j, lambda: tn(s.a1[...], dqkv[...]).astype(BF16))
        for m in range(x.shape[0] // BLOCK):
            at = slice(m * BLOCK, (m + 1) * BLOCK)
            da1[at, :] += nt(dqkv[at, :], wqkv[j])
        return 0

    lax.fori_loop(0, wqkv.shape[0], backward, 0)
    norm_one_back(x, s.da2, da1, vecs, s.gvec, s.a1)
    grad_copy = pltpu.make_async_copy(s.a1, input_grad, s.local.at[1])
    grad_copy.start()
    comm.end()
    act_copy.wait()
    grad_copy.wait()


class Named:
    def __init__(self, names, refs):
        for name, ref in zip(names, refs):
            setattr(self, name, ref)


def layer_scratch(length, width):
    heads = width // HEAD
    wide, tall = (length, width), (width, length)
    return {
        "a1": pltpu.VMEM(wide, BF16),
        "k": pltpu.VMEM(wide, BF16),
        "v": pltpu.VMEM(wide, BF16),
        "q_t": pltpu.VMEM(tall, BF16),
        "k_t": pltpu.VMEM(tall, BF16),
        "v_t": pltpu.VMEM(tall, BF16),
        "o_t": pltpu.VMEM(tall, BF16),
        "lse": pltpu.VMEM((heads, 1, length), F32),
        "delta": pltpu.VMEM((heads, 1, length), F32),
        "x2": pltpu.VMEM(wide, F32),
        "a2": pltpu.VMEM(wide, BF16),
        "out_acc": pltpu.VMEM(wide, F32),
        "da2": pltpu.VMEM(wide, F32),
        "g_f": pltpu.VMEM(wide, BF16),
        "work": pltpu.VMEM((length, 2 * TILE), BF16),
        "dk_t": pltpu.VMEM((2 * HEAD, length), F32),
        "dv_t": pltpu.VMEM((2 * HEAD, length), F32),
        "gvec": pltpu.VMEM((VEC_ROWS, width), F32),
        "local": pltpu.SemaphoreType.DMA((2,)),
    }


class Plain:
    def __init__(self, outs, stage, sem):
        self.outs, self.stage, self.sem = outs, stage, sem

    def begin(self):
        pass

    need_qkv = need_hidden = need_out = lambda self, *args: None

    def put(self, stage, place, make):
        stage[...] = make()
        copy = pltpu.make_async_copy(stage, place, self.sem)
        copy.start()
        copy.wait()

    def give_up(self, t, make):
        self.put(self.stage[1], self.outs[2].at[t], make)

    def give_down(self, t, make):
        self.put(self.stage[2], self.outs[3].at[t], make)

    def give_out(self, make):
        self.put(self.stage[0], self.outs[1], make)

    def give_qkv(self, j, make):
        self.put(self.stage[0], self.outs[0].at[j], make)

    def end(self):
        pass


def plain_layer(lengths, task_of, task_tokens, x, grad_out, wqkv, wout, wup, wdn, vecs):
    length, width = x.shape
    scratch = layer_scratch(length, width)
    names = tuple(scratch)

    def kernel(*refs):
        (lens, of, tokens, x, g, wqkv, wout, wup, wdn, vecs) = refs[:10]
        act, input_grad, gqkv, gout, gup, gdn, gvec = refs[10:17]
        s = Named(names, refs[17 : 17 + len(names)])
        rest = refs[17 + len(names) :]
        comm = Plain((gqkv, gout, gup, gdn), rest[:3], rest[3])
        layer_body(comm, lens, of, tokens, x, g, act, input_grad, (wqkv, wout, wup, wdn, vecs), s)
        gvec[...] = s.gvec[...]

    smem = pl.BlockSpec(memory_space=pltpu.SMEM)
    vmem = pl.BlockSpec(memory_space=pltpu.VMEM)
    hbm = pl.BlockSpec(memory_space=pl.ANY)
    like = lambda a: jax.ShapeDtypeStruct(a.shape, BF16)
    return pl.pallas_call(
        kernel,
        out_shape=(
            like(x), like(x), like(wqkv), like(wout), like(wup), like(wdn),
            jax.ShapeDtypeStruct((VEC_ROWS, width), F32),
        ),
        in_specs=[smem] * 3 + [vmem] * 7,
        out_specs=(hbm,) * 6 + (vmem,),
        scratch_shapes=list(scratch.values())
        + [
            pltpu.VMEM((width, width), BF16),
            pltpu.VMEM((width, TILE), BF16),
            pltpu.VMEM((TILE, width), BF16),
            pltpu.SemaphoreType.DMA,
        ],
        compiler_params=pltpu.CompilerParams(vmem_limit_bytes=62 * 2**20),
        name="layer",
    )(lengths, task_of, task_tokens, x, grad_out, wqkv, wout, wup, wdn, vecs)


def pack_vectors(bias_q, bias_v, bias_out, bias_up, bias_down, gain_one, shift_one, gain_two, shift_two):
    width = bias_q.shape[0]
    rows = jnp.stack([bias_q, bias_v, bias_out, bias_down, gain_one, shift_one, gain_two, shift_two])
    tiles = jnp.pad(bias_up.reshape(-1, TILE), ((0, 0), (0, width - TILE)))
    rest = jnp.zeros((VEC_ROWS - rows.shape[0] - tiles.shape[0], width), BF16)
    return jnp.concatenate([rows, tiles, rest]).astype(F32)


def plain_body(
    tokens, grad_out, lengths, task_of, task_tokens, w_qkv, w_out, w_up, w_down,
    bias_q, bias_v, bias_out, bias_up, bias_down, gain_one, shift_one, gain_two, shift_two,
):
    gather = lambda a: lax.all_gather(a, "dp", axis=0, tiled=True)
    width = tokens.shape[2]
    chunks, tiles = width // BLOCK, w_up.shape[1] // TILE
    wqkv = gather(w_qkv).reshape(width, 3, chunks, BLOCK).transpose(2, 0, 1, 3)
    wqkv = wqkv.reshape(chunks, width, 3 * BLOCK)
    wup = gather(w_up).reshape(width, tiles, TILE).transpose(1, 0, 2)
    wdn = gather(w_down).reshape(tiles, TILE, width)
    vecs = pack_vectors(
        *(gather(a) for a in (bias_q, bias_v, bias_out, bias_up, bias_down, gain_one, shift_one, gain_two, shift_two))
    )
    act, input_grad, gqkv, gout, gup, gdn, gvec = plain_layer(
        lengths, task_of, task_tokens, tokens[0], grad_out[0], wqkv, gather(w_out), wup, wdn, vecs
    )
    gqkv = gqkv.reshape(chunks, width, 3, BLOCK).transpose(1, 2, 0, 3).reshape(width, 3 * width)
    gup = gup.transpose(1, 0, 2).reshape(width, -1)
    gdn = gdn.reshape(-1, width)
    vectors = [gvec[BQ], gvec[BV], gvec[BO], gvec[UP : UP + tiles, :TILE].reshape(-1), gvec[BD]]
    vectors += [gvec[G1], gvec[S1], gvec[G2], gvec[S2]]
    grads = [gqkv, gout, gup, gdn] + [a.astype(BF16) for a in vectors]
    shares = lax.psum_scatter(grads, "dp", scatter_dimension=0, tiled=True)
    summed = jax.tree.map(lambda a: a.astype(F32), lax.psum(shares, "grp"))
    return (act[None], input_grad[None], *summed)


MESH = pl.DeviceIdType.MESH


class Place:
    def __init__(self):
        z, d = lax.axis_index("grp"), lax.axis_index("dp")
        self.z, self.d = z, d
        self.core = lax.rem(d, 2)
        self.chip = d // 2
        x, y = lax.rem(self.chip, 2), d // 4
        self.d_core = d + 1 - 2 * self.core
        self.d_x = d + 2 - 4 * x
        self.d_y = d + 4 - 8 * y
        self.d_diag = self.d_x + 4 - 8 * y
        self.chip_x, self.chip_y, self.chip_diag = self.d_x // 2, self.d_y // 2, self.d_diag // 2
        self.on_core, self.on_x, self.on_y = ((z, e) for e in (self.d_core, self.d_x, self.d_y))
        self.outer = (z == 0) | (z == 3)
        self.inner = (z == 1) | (z == 2)
        self.to_inner = (1 + z // 3, d)
        self.to_outer = (3 * (z // 2), d)
        self.to_mid = (3 - z, d)


def remote(src, dst, sems, index, device):
    send, recv = sems
    return pltpu.make_async_remote_copy(
        src_ref=src, dst_ref=dst, send_sem=send.at[index], recv_sem=recv.at[index],
        device_id=device, device_id_type=MESH,
    )


class Gather:
    def __init__(self, here, full, sems):
        self.here, self.full, self.sems = here, full, sems
        self.count, rows, _ = full.shape
        self.rows = rows // 8

    def block(self, i, owner, half=None):
        rows = self.rows if half is None else self.rows // 2
        start = owner * self.rows + (0 if half is None else half * rows)
        return self.full.at[i, pl.ds(pl.multiple_of(start, 16), rows), :]

    def copy(self, i, n):
        p = self.here
        owner, half, device = (
            (p.d, None, p.on_x),
            (p.d, None, p.on_y),
            (p.d, None, p.on_core),
            (p.d_x, None, p.on_core),
            (p.d_x, 0, p.on_y),
            (p.d_y, None, p.on_core),
            (p.d_y, 1, p.on_x),
            (p.d_diag, None, p.on_core),
        )[n]
        part = self.block(i, owner, half)
        return remote(part, part, self.sems, (n, i), device)

    def landed(self, i, n):
        p = self.here
        flip = 1 - 2 * p.core
        owner, half = (
            (p.d_x, None),
            (p.d_y, None),
            (p.d_core, None),
            (p.d_x + flip, None),
            (p.d_diag, 0),
            (p.d_y + flip, None),
            (p.d_diag, 1),
            (p.d_diag + flip, None),
        )[n]
        part = self.block(i, owner, half)
        remote(part, part, self.sems, (n, i), p.on_core).wait_recv()

    def start(self, i):
        for n in (0, 1, 2):
            self.copy(i, n).start()

    def relay(self, i):
        self.landed(i, 0)
        self.copy(i, 4).start()
        self.copy(i, 3).start()
        self.landed(i, 1)
        self.copy(i, 6).start()
        self.copy(i, 5).start()

    def diag(self, i):
        self.landed(i, 4)
        self.landed(i, 6)
        self.copy(i, 7).start()

    def need(self, i):
        for n in (2, 3, 5, 7):
            self.landed(i, n)

    def drain(self):
        def step(i, _):
            for n in range(8):
                self.copy(i, n).wait_send()
            return 0

        lax.fori_loop(0, self.count, step, 0)


def added(*refs_at):
    total = refs_at[0].astype(F32)
    for value in refs_at[1:]:
        total = total + value.astype(F32)
    return total.astype(BF16)


class Reduce:
    STAGES = 7

    def __init__(self, here, bufs, sems):
        self.here, self.sems = here, sems
        (self.sums, self.from_core, self.half_x, self.half_y, self.from_x, self.from_y,
         self.run, self.from_outer, self.from_mid, self.total) = bufs
        self.count, self.rows, self.columns = self.total.shape
        self.slots, self.run_slots = self.sums.shape[0] - 1, self.run.shape[0]
        self.outer_slots = self.from_outer.shape[0]

    @staticmethod
    def buffers(count, rows, columns, slots, run_slots):
        piece = (rows, columns)
        shapes = [(slots + 1, 4) + piece, (2, 4) + piece]
        shapes += [(2, rows // 2, columns)] * 2 + [(2,) + piece] * 2
        shapes += [(run_slots,) + piece, (run_slots,) + piece, (2,) + piece, (count,) + piece]
        return [pltpu.VMEM(shape, BF16) for shape in shapes]

    def mine(self, i):
        return 1 + lax.rem(i, self.slots)

    def copy(self, i, n):
        p, two, half = self.here, lax.rem(i, 2), self.rows // 2
        own = self.mine(i)
        run = self.run.at[lax.rem(i, self.run_slots)]
        src, dst, device = (
            lambda: (self.sums.at[0], self.from_core.at[two], p.on_core),
            lambda: (self.sums.at[own, p.chip_diag, :half], self.half_x.at[two], p.on_x),
            lambda: (self.sums.at[own, p.chip_diag, half:], self.half_y.at[two], p.on_y),
            lambda: (self.sums.at[own, p.chip_x], self.from_x.at[two], p.on_x),
            lambda: (self.sums.at[own, p.chip_y], self.from_y.at[two], p.on_y),
            lambda: (run, self.from_outer.at[lax.rem(i, self.outer_slots)], p.to_inner),
            lambda: (run, self.from_mid.at[two], p.to_mid),
            lambda: (self.total.at[i], self.total.at[i], p.to_outer),
        )[n]()
        return remote(src, dst, self.sems, (n, i), device)

    def stage_0(self, i, value):
        own, rows = self.mine(i), self.rows
        for owner in range(8):
            same = 1 - lax.rem(self.here.core + owner, 2)
            self.sums[same * own, owner // 2] = value[owner * rows : (owner + 1) * rows]
        self.copy(i, 0).start()

    def stage_1(self, i):
        own, two = self.mine(i), lax.rem(i, 2)
        done = self.copy(i, 0)
        done.wait_recv()
        done.wait_send()
        order = (self.here.chip_diag, self.here.chip_x, self.here.chip_y, self.here.chip)
        for n, chip in enumerate(order):
            self.sums[own, chip] = added(self.sums[own, chip], self.from_core[two, chip])
            if n == 0:
                self.copy(i, 1).start()
                self.copy(i, 2).start()

    def stage_2(self, i):
        p, own, two, half = self.here, self.mine(i), lax.rem(i, 2), self.rows // 2
        self.copy(i, 1).wait_recv()
        self.sums[own, p.chip_y, :half] = added(self.sums[own, p.chip_y, :half], self.half_x[two])
        self.copy(i, 4).start()
        self.copy(i, 2).wait_recv()
        self.sums[own, p.chip_x, half:] = added(self.sums[own, p.chip_x, half:], self.half_y[two])
        self.copy(i, 3).start()

    def stage_3(self, i):
        p, own, two = self.here, self.mine(i), lax.rem(i, 2)
        self.copy(i, 3).wait_recv()
        self.copy(i, 4).wait_recv()
        self.run[lax.rem(i, self.run_slots)] = added(
            self.sums[own, p.chip], self.from_x[two], self.from_y[two]
        )
        for n in (1, 2, 3, 4):
            self.copy(i, n).wait_send()
        pl.when(p.outer)(lambda: self.copy(i, 5).start())

    def stage_4(self, i):
        def work():
            self.copy(i, 5).wait_recv()
            at = lax.rem(i, self.run_slots)
            self.run[at] = added(self.run[at], self.from_outer[lax.rem(i, self.outer_slots)])
            self.copy(i, 6).start()

        pl.when(self.here.inner)(work)

    def stage_5(self, i):
        def work():
            self.copy(i, 6).wait_recv()
            self.total[i] = added(self.run[lax.rem(i, self.run_slots)], self.from_mid[lax.rem(i, 2)])
            self.copy(i, 7).start()

        pl.when(self.here.inner)(work)

    def stage_6(self, i):
        def finish_inner():
            self.copy(i, 6).wait_send()
            self.copy(i, 7).wait_send()

        def finish_outer():
            self.copy(i, 5).wait_send()
            self.copy(i, 7).wait_recv()

        pl.when(self.here.inner)(finish_inner)
        pl.when(self.here.outer)(finish_outer)

    def stage(self, s, i):
        getattr(self, "stage_%d" % s)(i)

    def guarded(self, s, i):
        pl.when((i >= 0) & (i < self.count))(lambda: self.stage(s, i))


class Fused:
    def __init__(self, here, ins, outs, g, c):
        self.here, self.ins, self.outs, self.g, self.c = here, ins, outs, g, c
        self.gather = {
            kind: Gather(here, g[kind], (c["g_send_" + kind], c["g_recv_" + kind])) for kind in "qud"
        }
        self.reduce = {
            kind: Reduce(here, c["r_" + kind], (c["r_send_" + kind], c["r_recv_" + kind]))
            for kind in "qud"
        }

    def greet(self):
        p, barrier = self.here, pltpu.get_barrier_semaphore()
        for step in range(1, 8):
            pl.semaphore_signal(
                barrier, inc=1, device_id=(p.z, lax.rem(p.d + step, 8)), device_id_type=MESH
            )
        for step in range(1, 4):
            pl.semaphore_signal(
                barrier, inc=1, device_id=(lax.rem(p.z + step, 4), p.d), device_id_type=MESH
            )
        pl.semaphore_wait(barrier, 10)

    def vector_copy(self, kind, step):
        p, c = self.here, self.c
        sems = (c["v_send"], c["v_recv"])
        if kind == 2:
            device = (lax.rem(p.z + step, 4), p.d)
            return remote(c["vz"].at[p.z], c["vz"].at[p.z], sems, (kind, step), device)
        device = (p.z, lax.rem(p.d + step, 8))
        if kind == 0:
            return remote(self.ins["vec"], c["vfull"].at[p.d], sems, (kind, step), device)
        return remote(c["vpack"].at[device[1]], c["vin"].at[step], sems, (kind, step), device)

    def vector_landed(self, kind, step):
        p, c = self.here, self.c
        sems = (c["v_send"], c["v_recv"])
        if kind == 2:
            part = c["vz"].at[lax.rem(p.z + 4 - step, 4)]
        elif kind == 0:
            part = c["vfull"].at[lax.rem(p.d + 8 - step, 8)]
        else:
            part = c["vin"].at[step]
        remote(part, part, sems, (kind, step), p.on_core).wait_recv()

    def own_copies(self):
        p, ins, g, sem = self.here, self.ins, self.g, self.c["own"]
        rows, width = ins["out"].shape
        parts = [[], [], [], [], []]
        at = pl.ds(pl.multiple_of(p.d * rows, 16), rows)
        for j in range(3):
            for part in range(3):
                src = ins["qkv"].at[:, pl.ds(part * width + j * BLOCK, BLOCK)]
                parts[j].append((src, g["q"].at[j, at, pl.ds(part * BLOCK, BLOCK)]))
        parts[3].append((ins["out"], g["q"].at[3, at, :]))
        for t in range(6):
            down = pl.ds(pl.multiple_of(p.d * 64, 16), 64)
            parts[4].append((ins["down"].at[pl.ds(64 * t, 64), :], g["d"].at[t, down, :]))
        copies = []
        for n, part in enumerate(parts):
            copies.append([pltpu.make_async_copy(src, dst, sem.at[n]) for src, dst in part])
        return copies

    def up_copies(self, room):
        rows = self.ins["up"].shape[0]
        return [
            pltpu.make_async_copy(
                self.ins["up"].at[:, pl.ds(1024 * b, 1024)],
                room.at[pl.ds(rows * b, rows), :],
                self.c["own"].at[5],
            )
            for b in range(3)
        ]

    def place_up(self, room):
        rows = self.ins["up"].shape[0]
        at = pl.ds(pl.multiple_of(self.here.d * rows, 16), rows)

        def piece(owner, t):
            start = 384 * owner + 64 * t
            block, off = start // 1024, start % 1024
            return room[block * rows : (block + 1) * rows, off : off + 64]

        for t in range(6):
            for pair in range(4):
                both = jnp.concatenate([piece(2 * pair, t), piece(2 * pair + 1, t)], axis=1)
                self.g["u"][t, at, 128 * pair : 128 * (pair + 1)] = both

    def spread_vectors(self, vecs):
        vfull = self.c["vfull"]
        vecs[...] = jnp.zeros_like(vecs)
        rows = self.ins["out"].shape[0]
        for owner in range(8):
            vecs[0:8, rows * owner : rows * (owner + 1)] = vfull[owner, 0:8, :rows]
            vecs[8:14, 64 * owner : 64 * (owner + 1)] = vfull[owner, 8:14, :64]

    def pack_vectors(self, gvec):
        vpack = self.c["vpack"]
        vpack[...] = jnp.zeros_like(vpack)
        rows = self.ins["out"].shape[0]
        for owner in range(8):
            vpack[owner, 0:8, :rows] = gvec[0:8, rows * owner : rows * (owner + 1)]
            vpack[owner, 8:14, :64] = gvec[8:14, 64 * owner : 64 * (owner + 1)]


def fused_body(comm, lengths, task_of, task_tokens, hbm_x, hbm_grad, act, input_grad, vecs, s):
    here, c, g = comm.here, comm.c, comm.g
    gq, gu, gd = (comm.gather[kind] for kind in "qud")
    rq, ru, rd = (comm.reduce[kind] for kind in "qud")
    wq, wup, wdn = g["q"], g["u"], g["d"]
    wout = wq.at[3]
    length_s = lengths[0]
    weight_s = task_weight(task_of, task_tokens)
    get_x = pltpu.make_async_copy(hbm_x, s.x, s.local.at[2])
    get_grad = pltpu.make_async_copy(hbm_grad, s.x, s.local.at[3])
    get_x_again = pltpu.make_async_copy(hbm_x, s.x, s.local.at[4])
    own = comm.own_copies()
    ups = comm.up_copies(s.o_t)
    own_vec = pltpu.make_async_copy(comm.ins["vec"], c["vfull"].at[here.d], c["own"].at[6])
    for copy in own[0] + [own_vec] + own[1] + own[2] + [get_x] + ups + own[3] + own[4]:
        copy.start()
    s.gvec[...] = jnp.zeros_like(s.gvec)
    s.da2[...] = jnp.zeros_like(s.da2)
    comm.greet()
    for step in range(1, 8):
        comm.vector_copy(0, step).start()
    for j in range(2):
        for copy in own[j]:
            copy.wait()
        gq.start(j)
    for copy in ups:
        copy.wait()
    comm.place_up(s.o_t)
    own_vec.wait()
    for step in range(1, 8):
        comm.vector_landed(0, step)
    comm.spread_vectors(vecs)
    get_x.wait()
    norm_one_phase(s.x, vecs, s.a1, s.x2)
    get_grad.start()
    gq.relay(0)
    for copy in own[2] + own[3] + own[4]:
        copy.wait()
    gq.diag(0)

    def hidden_start(t):
        gu.start(t)
        gd.start(t)

    def hidden_relay(t):
        gu.relay(t)
        gd.relay(t)

    def hidden_diag(t):
        gu.diag(t)
        gd.diag(t)

    def forward(j, _):
        pl.when(j < 2)(lambda: gq.start(j + 2))
        pl.when(j == 2)(lambda: hidden_start(0))
        gq.need(j)
        qkv_phase(j, s.a1, wq, vecs, s.k, s.v, s.q_t, s.k_t, s.v_t)
        gq.relay(j + 1)

        def pair(n, _):
            attend_pair(2 * j + n, length_s, s.k, s.q_t, s.v_t, s.o_t, s.lse)
            pl.when(n == 0)(lambda: gq.diag(j + 1))
            return 0

        return lax.fori_loop(0, 2, pair, 0)

    lax.fori_loop(0, 3, forward, 0)
    hidden_start(1)
    hidden_relay(0)
    get_grad.wait()
    branch_phase(s.x, length_s, weight_s, s.g_f, s.gvec)
    gq.need(3)
    norm_two_phase(s.o_t, wout, vecs, s.x2, s.a2, s.out_acc)
    hidden_diag(0)
    hr, gu_tile = s.work.at[:, :TILE], s.work.at[:, TILE:]

    def hidden(t, _):
        pl.when(t < 4)(lambda: hidden_start(t + 2))
        gu.need(t)
        gd.need(t)
        hidden_tile(t, s.a2, s.g_f, wup, wdn, vecs, s.out_acc, s.da2, hr, gu_tile, s.gvec)
        pl.when(t < 5)(lambda: hidden_relay(t + 1))
        for stage in range(6, 0, -1):
            ru.guarded(stage, t - stage)
            rd.guarded(stage, t - stage)
        ru.stage_0(t, tn(s.a2[...], gu_tile[...]).astype(BF16))
        rd.stage_0(t, tn(hr[...], s.g_f[...]).astype(BF16))
        pl.when(t < 5)(lambda: hidden_diag(t + 1))
        return 0

    lax.fori_loop(0, 6, hidden, 0)

    def hidden_point(step):
        for stage in range(6, 0, -1):
            item = step - stage
            if isinstance(step, int):
                if 0 <= item < 6:
                    ru.stage(stage, item)
                    rd.stage(stage, item)
            else:
                ru.guarded(stage, item)
                rd.guarded(stage, item)

    norm_two_back(s.x, length_s, weight_s, s.x2, s.da2, vecs, s.a2, s.gvec, s.out_acc, s.g_f)
    get_x_again.start()
    act_copy = pltpu.make_async_copy(s.g_f, act, s.local.at[0])
    act_copy.start()
    hidden_point(6)
    rq.stage_0(0, nn(s.o_t[...], s.a2[...]).astype(BF16))
    g_o_t = s.v_t
    attended_back(wout, s.a2, s.o_t, g_o_t, s.delta)
    hidden_point(7)
    da1 = s.out_acc
    da1[...] = jnp.zeros_like(da1)
    dqkv = s.work.at[:, : 3 * BLOCK]

    def backward(j, _):
        def pair(n, _):
            attend_back_pair(
                2 * j + n, s.k, s.v, s.q_t, s.k_t, g_o_t, s.lse, s.delta,
                s.dk_t, s.dv_t, dqkv, s.gvec,
            )
            hidden_point(8 + 2 * j + n)

            def even():
                rq.guarded(5, j - 2)
                rq.guarded(3, j - 1)
                rq.stage(1, j)

            def odd():
                rq.guarded(6, j - 2)
                rq.guarded(4, j - 1)
                rq.stage(2, j)

            pl.when(n == 0)(even)
            pl.when(n == 1)(odd)
            return 0

        lax.fori_loop(0, 2, pair, 0)
        rq.stage_0(j + 1, tn(s.a1[...], dqkv[...]).astype(BF16))
        for m in range(s.x.shape[0] // BLOCK):
            at = slice(m * BLOCK, (m + 1) * BLOCK)
            da1[at, :] += nt(dqkv[at, :], wq[j])
        return 0

    lax.fori_loop(0, 3, backward, 0)
    get_x_again.wait()
    rq.stage(5, 1)
    rq.stage(3, 2)
    rq.stage(1, 3)
    norm_one_back(s.x, s.da2, da1, vecs, s.gvec, s.a1)
    grad_copy = pltpu.make_async_copy(s.a1, input_grad, s.local.at[1])
    grad_copy.start()
    comm.pack_vectors(s.gvec)
    for step in range(1, 8):
        comm.vector_copy(1, step).start()
    rq.stage(6, 1)
    rq.stage(4, 2)
    rq.stage(2, 3)
    outs = comm.outs
    rows = comm.ins["out"].shape[0]
    width = s.x.shape[1]
    x2 = s.x2
    x2[:rows, :] = rq.total[0].astype(F32)
    copies = [pltpu.make_async_copy(x2.at[pl.ds(0, rows), :], outs["out"], s.local.at[5])]
    copies[0].start()
    for t in range(6):
        x2[rows + 64 * t : rows + 64 * (t + 1), :] = rd.total[t].astype(F32)
    copies.append(pltpu.make_async_copy(x2.at[pl.ds(rows, 384), :], outs["down"], s.local.at[6]))
    copies[1].start()
    base = rows + 384
    for group in range(24):
        owner, t = group // 3, 2 * (group % 3)
        lanes = slice(64 * owner, 64 * (owner + 1))
        both = jnp.concatenate([ru.total[t, :, lanes], ru.total[t + 1, :, lanes]], axis=1)
        at, off = base + rows * (group // 6), 128 * (group % 6)
        x2[at : at + rows, off : off + 128] = both.astype(F32)
    for b in range(4):
        copies.append(
            pltpu.make_async_copy(
                x2.at[pl.ds(base + rows * b, rows), :],
                outs["up"].at[:, pl.ds(width * b, width)],
                s.local.at[7 + b],
            )
        )
        copies[-1].start()
    for step in range(1, 8):
        comm.vector_landed(1, step)
    share = c["vpack"][here.d]
    for step in range(1, 8):
        share = share + c["vin"][step]
    c["vz"][here.z] = share
    for step in range(1, 4):
        comm.vector_copy(2, step).start()
    rq.stage(5, 2)
    rq.stage(3, 3)

    def out_qkv(j):
        for part in range(3):
            da1[part * rows : (part + 1) * rows, j * BLOCK : (j + 1) * BLOCK] = rq.total[
                j + 1, :, part * BLOCK : (part + 1) * BLOCK
            ].astype(F32)

    out_qkv(0)
    rq.stage(6, 2)
    rq.stage(4, 3)
    out_qkv(1)
    for step in range(1, 4):
        comm.vector_landed(2, step)
    vz = c["vz"]
    outs["vec"][...] = (vz[0] + vz[1]) + (vz[2] + vz[3])
    gq.drain()
    gu.drain()
    gd.drain()
    for kind, count in ((0, 8), (1, 8), (2, 4)):
        for step in range(1, count):
            comm.vector_copy(kind, step).wait_send()
    rq.stage(5, 3)
    rq.stage(6, 3)
    out_qkv(2)
    for part in range(3):
        copies.append(
            pltpu.make_async_copy(
                da1.at[pl.ds(part * rows, rows), :],
                outs["qkv"].at[:, pl.ds(width * part, width)],
                s.local.at[11 + part],
            )
        )
        copies[-1].start()
    act_copy.wait()
    grad_copy.wait()
    for copy in copies:
        copy.wait()


def fused_layer(lengths, task_of, task_tokens, x, grad_out, w_qkv, w_out, w_up, w_down, vec):
    length, width = x.shape
    rows = w_out.shape[0]
    shapes = layer_scratch(length, width)
    shapes["x"] = pltpu.VMEM((length, width), BF16)
    shapes["vecs"] = pltpu.VMEM((VEC_ROWS, width), F32)
    shapes["local"] = pltpu.SemaphoreType.DMA((14,))
    full = {
        "q": pltpu.VMEM((4, width, width), BF16),
        "u": pltpu.VMEM((6, width, TILE), BF16),
        "d": pltpu.VMEM((6, TILE, width), BF16),
    }
    comm_shapes = {
        "own": pltpu.SemaphoreType.DMA((7,)),
        "v_send": pltpu.SemaphoreType.DMA((3, 8)),
        "v_recv": pltpu.SemaphoreType.DMA((3, 8)),
        "vfull": pltpu.VMEM((8, VEC_ROWS, 128), F32),
        "vpack": pltpu.VMEM((8, VEC_ROWS, 128), F32),
        "vin": pltpu.VMEM((8, VEC_ROWS, 128), F32),
        "vz": pltpu.VMEM((4, VEC_ROWS, 128), F32),
    }
    for kind, count in (("q", 4), ("u", 6), ("d", 6)):
        for name in ("g_send_", "g_recv_", "r_send_", "r_recv_"):
            comm_shapes[name + kind] = pltpu.SemaphoreType.DMA((8, count))
    sums = {
        "q": Reduce.buffers(4, rows, width, 2, 2),
        "u": Reduce.buffers(6, rows, TILE, 3, 3),
        "d": Reduce.buffers(6, 64, width, 3, 3),
    }
    names, comm_names = tuple(shapes), tuple(comm_shapes)
    scratch = list(shapes.values()) + list(full.values()) + list(comm_shapes.values())
    for kind in "qud":
        scratch += sums[kind]

    def kernel(*refs):
        refs = list(refs)
        take = lambda n: [refs.pop(0) for _ in range(n)]
        lens, of, tokens, hbm_x, hbm_grad = take(5)
        ins = dict(zip(("qkv", "out", "up", "down", "vec"), take(5)))
        act, input_grad = take(2)
        outs = dict(zip(("qkv", "out", "up", "down", "vec"), take(5)))
        s = Named(names, take(len(names)))
        g = dict(zip("qud", take(3)))
        c = dict(zip(comm_names, take(len(comm_names))))
        for kind in "qud":
            c["r_" + kind] = take(10)
        comm = Fused(Place(), ins, outs, g, c)
        fused_body(comm, lens, of, tokens, hbm_x, hbm_grad, act, input_grad, s.vecs, s)

    smem = pl.BlockSpec(memory_space=pltpu.SMEM)
    vmem = pl.BlockSpec(memory_space=pltpu.VMEM)
    hbm = pl.BlockSpec(memory_space=pl.ANY)
    like = lambda a: jax.ShapeDtypeStruct(a.shape, F32)
    return pl.pallas_call(
        kernel,
        out_shape=(
            jax.ShapeDtypeStruct(x.shape, BF16), jax.ShapeDtypeStruct(x.shape, BF16),
            like(w_qkv), like(w_out), like(w_up), like(w_down), like(vec),
        ),
        in_specs=[smem] * 3 + [hbm] * 6 + [vmem],
        out_specs=(hbm,) * 6 + (vmem,),
        scratch_shapes=scratch,
        compiler_params=pltpu.CompilerParams(
            vmem_limit_bytes=63 * 2**20, collective_id=0, has_side_effects=True
        ),
        name="layer",
    )(lengths, task_of, task_tokens, x, grad_out, w_qkv, w_out, w_up, w_down, vec)


def fused_shards(
    tokens, grad_out, lengths, task_of, task_tokens, w_qkv, w_out, w_up, w_down,
    bias_q, bias_v, bias_out, bias_up, bias_down, gain_one, shift_one, gain_two, shift_two,
):
    rows = w_out.shape[0]
    eight = jnp.stack([bias_q, bias_v, bias_out, bias_down, gain_one, shift_one, gain_two, shift_two])
    up = bias_up.reshape(6, 64)
    vec = jnp.concatenate(
        [
            jnp.pad(eight, ((0, 0), (0, 128 - rows))),
            jnp.pad(up, ((0, VEC_ROWS - 8 - 6), (0, 64))),
        ]
    ).astype(F32)
    act, input_grad, gqkv, gout, gup, gdn, gvec = fused_layer(
        lengths, task_of, task_tokens, tokens[0], grad_out[0], w_qkv, w_out, w_up, w_down, vec
    )
    line = lambda n: gvec[n, :rows]
    return (
        act[None], input_grad[None], gqkv, gout, gup, gdn, line(BQ), line(BV), line(BO),
        gvec[UP : UP + 6, :64].reshape(-1), line(BD), line(G1), line(S1), line(G2), line(S2),
    )


def solution(mesh):
    rows = P(("grp", "dp"), None, None)
    each = P(("grp", "dp"))
    matrix, vector = P("dp", None), P("dp")
    in_specs = (rows, rows, each, each, P()) + (matrix,) * 4 + (vector,) * 9
    out_specs = (rows, rows) + (matrix,) * 4 + (vector,) * 9
    small = mesh.shape["dp"] == 8 and mesh.shape["grp"] == 4
    body = fused_shards if small else plain_body
    return jax.shard_map(body, mesh=mesh, in_specs=in_specs, out_specs=out_specs, check_vma=False)
```

```python
import functools
import math

import jax
import jax.numpy as jnp
from jax import lax
from jax.experimental import pallas as pl
from jax.experimental.pallas import tpu as pltpu
from jax.sharding import PartitionSpec as P

F32 = jnp.float32
BF16 = jnp.bfloat16
EPS = 1e-05
UNIT = 1024.0
HEAD = 64
BLOCK = 256
TILE = 512
BQ, BV, BO, BD, G1, S1, G2, S2, UP = range(9)
VEC_ROWS = 16


def dot(left, right, left_dim, right_dim):
    return lax.dot_general(
        left, right, (((left_dim,), (right_dim,)), ((), ())), preferred_element_type=F32
    )


def nn(left, right):
    return dot(left, right, 1, 0)


def nt(left, right):
    return dot(left, right, 1, 1)


def tn(left, right):
    return dot(left, right, 0, 0)


def norm_rows(values):
    mean = jnp.mean(values, axis=-1, keepdims=True)
    centered = values - mean
    rstd = lax.rsqrt(jnp.mean(centered * centered, axis=-1, keepdims=True) + EPS)
    return centered * rstd, rstd


def norm_back(grad_norm, normed, rstd):
    mean_one = jnp.mean(grad_norm, axis=-1, keepdims=True)
    mean_two = jnp.mean(grad_norm * normed, axis=-1, keepdims=True)
    return rstd * (grad_norm - mean_one - normed * mean_two)


def column_sum(values):
    return jnp.sum(values, axis=0, keepdims=True)


def rows_at(index, size=BLOCK):
    return pl.ds(pl.multiple_of(index * size, size), size)


def norm_one_phase(x, vecs, a1, x2):
    gain, shift = vecs[G1 : G1 + 1, :], vecs[S1 : S1 + 1, :]

    def step(i, _):
        at = rows_at(i)
        value = x[at, :].astype(F32)
        x2[at, :] = value
        normed, _ = norm_rows(value)
        a1[at, :] = (normed * gain + shift).astype(BF16)
        return 0

    lax.fori_loop(0, x.shape[0] // BLOCK, step, 0)


def qkv_phase(j, a1, wqkv, vecs, k, v, q_t, k_t, v_t):
    at = rows_at(j)
    values = nn(a1[...], wqkv[j])
    bias_q, bias_v = vecs[BQ : BQ + 1, at], vecs[BV : BV + 1, at]
    query = (values[:, :BLOCK] + bias_q).astype(BF16) * (HEAD**-0.5)
    key_all = values[:, BLOCK : 2 * BLOCK].astype(BF16)
    value = (values[:, 2 * BLOCK :] + bias_v).astype(BF16)
    k[:, at] = key_all
    v[:, at] = value
    q_t[at, :] = query.T
    k_t[at, :] = key_all.T
    v_t[at, :] = value.T


def padded(rows, side):
    zeros = jnp.zeros_like(rows)
    return jnp.concatenate([rows, zeros] if side == 0 else [zeros, rows], axis=0)


def attend_pair(p, length_s, k, q_t, v_t, o_t, lse):
    length = k.shape[0]
    lanes = rows_at(p, 2 * HEAD)
    for i in range(length // BLOCK):
        cols = slice(i * BLOCK, (i + 1) * BLOCK)
        seen = (i + 1) * BLOCK
        queries = i * BLOCK + lax.broadcasted_iota(jnp.int32, (1, BLOCK), 1)
        limit = jnp.minimum(queries + 1, length_s)
        key_index = lax.broadcasted_iota(jnp.int32, (seen, BLOCK), 0)
        allowed = key_index < limit
        halves = []
        for side in range(2):
            head = 2 * p + side
            at = rows_at(head, HEAD)
            scores = nn(k[:seen, lanes], padded(q_t[at, cols], side))
            scores = jnp.where(allowed, scores, -1e30)
            top = jnp.max(scores, axis=0, keepdims=True)
            weights = jnp.exp(scores - top)
            total = jnp.sum(weights, axis=0, keepdims=True)
            lse[head, :, cols] = jnp.where(queries < length_s, top + jnp.log(total), 1e30)
            result = nn(v_t[at, :seen], weights.astype(BF16)) * (1.0 / total)
            halves.append(result.astype(BF16))
        o_t[lanes, cols] = jnp.concatenate(halves, axis=0)


def attend_back_pair(p, k, v, q_t, k_t, g_o_t, lse, delta, dk_t, dv_t, dqkv, gvec):
    length = k.shape[0]
    count = length // BLOCK
    lanes = rows_at(p, 2 * HEAD)
    dq_sides = []
    for side in range(2):
        head = 2 * p + side
        at = rows_at(head, HEAD)
        here = slice(side * HEAD, (side + 1) * HEAD)
        dq_parts = []
        for i in reversed(range(count)):
            cols = slice(i * BLOCK, (i + 1) * BLOCK)
            seen = (i + 1) * BLOCK
            q_cols, g_cols = q_t[at, cols], g_o_t[at, cols]
            scores = nn(k[:seen, lanes], padded(q_cols, side))
            key_index = lax.broadcasted_iota(jnp.int32, (BLOCK, BLOCK), 0)
            query_index = lax.broadcasted_iota(jnp.int32, (BLOCK, BLOCK), 1)
            diagonal = jnp.where(key_index <= query_index, scores[seen - BLOCK :], -1e30)
            if i > 0:
                scores = jnp.concatenate([scores[: seen - BLOCK], diagonal], axis=0)
            else:
                scores = diagonal
            probs = jnp.exp(scores - lse[head, :, cols])
            grad_probs = nn(v[:seen, lanes], padded(g_cols, side))
            grad_scores = (probs * (grad_probs - delta[head, :, cols])).astype(BF16)
            part_v = nt(g_cols, probs.astype(BF16))
            part_k = nt(q_cols, grad_scores)
            if i == count - 1:
                dv_t[here, :] = part_v
                dk_t[here, :] = part_k
            else:
                dv_t[here, :seen] += part_v
                dk_t[here, :seen] += part_k
            dq_parts.append(nn(k_t[at, :seen], grad_scores) * (HEAD**-0.5))
        dq_sides.append(jnp.concatenate(dq_parts[::-1], axis=1).astype(BF16))
    dq = jnp.concatenate(dq_sides, axis=0).T
    dk = dk_t[...].astype(BF16).T
    dv = dv_t[...].astype(BF16).T
    base = lax.rem(p, 2) * (2 * HEAD)
    for part, value in enumerate((dq, dk, dv)):
        place = pl.ds(pl.multiple_of(base + part * BLOCK, 2 * HEAD), 2 * HEAD)
        dqkv[:, place] = value
    gvec[BQ : BQ + 1, lanes] = column_sum(dq.astype(F32))
    gvec[BV : BV + 1, lanes] = column_sum(dv.astype(F32))


def norm_two_phase(o_t, wout, vecs, x2, a2, out_acc):
    bias, down = vecs[BO : BO + 1, :], vecs[BD : BD + 1, :]
    gain, shift = vecs[G2 : G2 + 1, :], vecs[S2 : S2 + 1, :]

    for i in range(x2.shape[0] // BLOCK):
        at = slice(i * BLOCK, (i + 1) * BLOCK)
        value = x2[at, :] + tn(o_t[:, at], wout[...]) + bias
        x2[at, :] = value
        out_acc[at, :] = value + down
        normed, _ = norm_rows(value)
        a2[at, :] = (normed * gain + shift).astype(BF16)


def cotangent_rows(i, grad_out, length_s, weight_s):
    at = rows_at(i)
    index = i * BLOCK + lax.broadcasted_iota(jnp.int32, (BLOCK, 1), 0)
    scale = jnp.where(index < length_s, weight_s, 0.0)
    return grad_out[at, :].astype(F32) * scale


def branch_phase(grad_out, length_s, weight_s, g_f, gvec):
    def step(i, total):
        rounded = cotangent_rows(i, grad_out, length_s, weight_s).astype(BF16)
        g_f[rows_at(i), :] = rounded
        return total + column_sum(rounded.astype(F32))

    width = grad_out.shape[1]
    total = lax.fori_loop(0, grad_out.shape[0] // BLOCK, step, jnp.zeros((1, width), F32))
    gvec[BD : BD + 1, :] = total


def hidden_tile(t, a2, g_f, wup, wdn, vecs, out_acc, da2, hr, gu, gvec):
    length = a2.shape[0]
    up, down = wup[t], wdn[t]
    bias = vecs[pl.ds(UP + t, 1), :TILE]
    total = jnp.zeros((1, TILE), F32)
    for m in range(length // BLOCK):
        at = slice(m * BLOCK, (m + 1) * BLOCK)
        u = nn(a2[at, :], up) + bias
        dh = nt(g_f[at, :], down)
        cdf = 0.5 + 0.5 * lax.erf(u * (1.0 / math.sqrt(2.0)))
        slope = cdf + u * (jnp.exp(-0.5 * u * u) * (1.0 / math.sqrt(2.0 * math.pi)))
        hidden = (u * cdf).astype(BF16)
        g_u = (dh * slope).astype(BF16)
        hr[at, :] = hidden
        gu[at, :] = g_u
        total = total + column_sum(g_u.astype(F32))
        out_acc[at, :] += nn(hidden, down)
        da2[at, :] += nt(g_u, up)
    gvec[pl.ds(UP + t, 1), :TILE] = total


def norm_two_back(grad_out, length_s, weight_s, x2, da2, vecs, g_a, gvec, out_acc, act):
    gain = vecs[G2 : G2 + 1, :]
    width = x2.shape[1]

    def step(i, carry):
        at = rows_at(i)
        act[at, :] = out_acc[at, :].astype(BF16)
        normed, rstd = norm_rows(x2[at, :])
        grad = da2[at, :]
        dx2 = cotangent_rows(i, grad_out, length_s, weight_s) + norm_back(grad * gain, normed, rstd)
        da2[at, :] = dx2
        rounded = dx2.astype(BF16)
        g_a[at, :] = rounded
        return (
            carry[0] + column_sum(grad * normed),
            carry[1] + column_sum(grad),
            carry[2] + column_sum(rounded.astype(F32)),
        )

    zero = jnp.zeros((1, width), F32)
    sums = lax.fori_loop(0, x2.shape[0] // BLOCK, step, (zero, zero, zero))
    gvec[G2 : G2 + 1, :], gvec[S2 : S2 + 1, :], gvec[BO : BO + 1, :] = sums


def attended_back(wout, g_a, o_t, g_o_t, delta):
    for i in range(g_a.shape[0] // BLOCK):
        cols = slice(i * BLOCK, (i + 1) * BLOCK)
        grad = nt(wout[...], g_a[cols, :]).astype(BF16)
        g_o_t[:, cols] = grad
        product = grad.astype(F32) * o_t[:, cols].astype(F32)
        for head in range(wout.shape[0] // HEAD):
            delta[head, :, cols] = column_sum(product[head * HEAD : (head + 1) * HEAD])


def norm_one_back(x, dx2, da1, vecs, gvec, input_grad):
    gain = vecs[G1 : G1 + 1, :]
    width = x.shape[1]

    def step(i, carry):
        at = rows_at(i)
        normed, rstd = norm_rows(x[at, :].astype(F32))
        grad = da1[at, :]
        result = dx2[at, :] + norm_back(grad * gain, normed, rstd)
        input_grad[at, :] = result.astype(BF16)
        return (carry[0] + column_sum(grad * normed), carry[1] + column_sum(grad))

    zero = jnp.zeros((1, width), F32)
    sums = lax.fori_loop(0, x.shape[0] // BLOCK, step, (zero, zero))
    gvec[G1 : G1 + 1, :], gvec[S1 : S1 + 1, :] = sums


def task_weight(task_of, task_tokens):
    return UNIT / task_tokens[task_of[0]].astype(F32)


def layer_body(comm, lengths, task_of, task_tokens, x, grad_out, act, input_grad, w, s):
    length_s = lengths[0]
    weight_s = task_weight(task_of, task_tokens)
    wqkv, wout, wup, wdn, vecs = w
    s.gvec[...] = jnp.zeros_like(s.gvec)
    s.da2[...] = jnp.zeros_like(s.da2)
    comm.begin()
    norm_one_phase(x, vecs, s.a1, s.x2)
    branch_phase(grad_out, length_s, weight_s, s.g_f, s.gvec)

    def forward(j, _):
        comm.need_qkv(j)
        qkv_phase(j, s.a1, wqkv, vecs, s.k, s.v, s.q_t, s.k_t, s.v_t)

        def pair(p, _):
            attend_pair(2 * j + p, length_s, s.k, s.q_t, s.v_t, s.o_t, s.lse)
            return 0

        return lax.fori_loop(0, 2, pair, 0)

    lax.fori_loop(0, wqkv.shape[0], forward, 0)
    comm.need_out()
    norm_two_phase(s.o_t, wout, vecs, s.x2, s.a2, s.out_acc)

    hr, gu, dqkv = s.work.at[:, :TILE], s.work.at[:, TILE:], s.work.at[:, : 3 * BLOCK]
    g_o_t = s.v_t

    def hidden(t, _):
        comm.need_hidden(t)
        hidden_tile(t, s.a2, s.g_f, wup, wdn, vecs, s.out_acc, s.da2, hr, gu, s.gvec)
        comm.give_up(t, lambda: tn(s.a2[...], gu[...]).astype(BF16))
        comm.give_down(t, lambda: tn(hr[...], s.g_f[...]).astype(BF16))
        return 0

    lax.fori_loop(0, wup.shape[0], hidden, 0)
    norm_two_back(
        grad_out, length_s, weight_s, s.x2, s.da2, vecs, s.a2, s.gvec, s.out_acc, s.g_f
    )
    act_copy = pltpu.make_async_copy(s.g_f, act, s.local.at[0])
    act_copy.start()
    comm.give_out(lambda: nn(s.o_t[...], s.a2[...]).astype(BF16))
    attended_back(wout, s.a2, s.o_t, g_o_t, s.delta)
    da1 = s.out_acc
    da1[...] = jnp.zeros_like(da1)

    def backward(j, _):
        def pair(p, _):
            attend_back_pair(
                2 * j + p, s.k, s.v, s.q_t, s.k_t, g_o_t, s.lse, s.delta,
                s.dk_t, s.dv_t, dqkv, s.gvec,
            )
            return 0

        lax.fori_loop(0, 2, pair, 0)
        comm.give_qkv(j, lambda: tn(s.a1[...], dqkv[...]).astype(BF16))
        for m in range(x.shape[0] // BLOCK):
            at = slice(m * BLOCK, (m + 1) * BLOCK)
            da1[at, :] += nt(dqkv[at, :], wqkv[j])
        return 0

    lax.fori_loop(0, wqkv.shape[0], backward, 0)
    norm_one_back(x, s.da2, da1, vecs, s.gvec, s.a1)
    grad_copy = pltpu.make_async_copy(s.a1, input_grad, s.local.at[1])
    grad_copy.start()
    comm.end()
    act_copy.wait()
    grad_copy.wait()


class Named:
    def __init__(self, names, refs):
        for name, ref in zip(names, refs):
            setattr(self, name, ref)


def layer_scratch(length, width):
    heads = width // HEAD
    wide, tall = (length, width), (width, length)
    return {
        "a1": pltpu.VMEM(wide, BF16),
        "k": pltpu.VMEM(wide, BF16),
        "v": pltpu.VMEM(wide, BF16),
        "q_t": pltpu.VMEM(tall, BF16),
        "k_t": pltpu.VMEM(tall, BF16),
        "v_t": pltpu.VMEM(tall, BF16),
        "o_t": pltpu.VMEM(tall, BF16),
        "lse": pltpu.VMEM((heads, 1, length), F32),
        "delta": pltpu.VMEM((heads, 1, length), F32),
        "x2": pltpu.VMEM(wide, F32),
        "a2": pltpu.VMEM(wide, BF16),
        "out_acc": pltpu.VMEM(wide, F32),
        "da2": pltpu.VMEM(wide, F32),
        "g_f": pltpu.VMEM(wide, BF16),
        "work": pltpu.VMEM((length, 2 * TILE), BF16),
        "dk_t": pltpu.VMEM((2 * HEAD, length), F32),
        "dv_t": pltpu.VMEM((2 * HEAD, length), F32),
        "gvec": pltpu.VMEM((VEC_ROWS, width), F32),
        "local": pltpu.SemaphoreType.DMA((2,)),
    }


class Plain:
    def __init__(self, outs, stage, sem):
        self.outs, self.stage, self.sem = outs, stage, sem

    def begin(self):
        pass

    need_qkv = need_hidden = need_out = lambda self, *args: None

    def put(self, stage, place, make):
        stage[...] = make()
        copy = pltpu.make_async_copy(stage, place, self.sem)
        copy.start()
        copy.wait()

    def give_up(self, t, make):
        self.put(self.stage[1], self.outs[2].at[t], make)

    def give_down(self, t, make):
        self.put(self.stage[2], self.outs[3].at[t], make)

    def give_out(self, make):
        self.put(self.stage[0], self.outs[1], make)

    def give_qkv(self, j, make):
        self.put(self.stage[0], self.outs[0].at[j], make)

    def end(self):
        pass


def plain_layer(lengths, task_of, task_tokens, x, grad_out, wqkv, wout, wup, wdn, vecs):
    length, width = x.shape
    scratch = layer_scratch(length, width)
    names = tuple(scratch)

    def kernel(*refs):
        (lens, of, tokens, x, g, wqkv, wout, wup, wdn, vecs) = refs[:10]
        act, input_grad, gqkv, gout, gup, gdn, gvec = refs[10:17]
        s = Named(names, refs[17 : 17 + len(names)])
        rest = refs[17 + len(names) :]
        comm = Plain((gqkv, gout, gup, gdn), rest[:3], rest[3])
        layer_body(comm, lens, of, tokens, x, g, act, input_grad, (wqkv, wout, wup, wdn, vecs), s)
        gvec[...] = s.gvec[...]

    smem = pl.BlockSpec(memory_space=pltpu.SMEM)
    vmem = pl.BlockSpec(memory_space=pltpu.VMEM)
    hbm = pl.BlockSpec(memory_space=pl.ANY)
    like = lambda a: jax.ShapeDtypeStruct(a.shape, BF16)
    return pl.pallas_call(
        kernel,
        out_shape=(
            like(x), like(x), like(wqkv), like(wout), like(wup), like(wdn),
            jax.ShapeDtypeStruct((VEC_ROWS, width), F32),
        ),
        in_specs=[smem] * 3 + [vmem] * 7,
        out_specs=(hbm,) * 6 + (vmem,),
        scratch_shapes=list(scratch.values())
        + [
            pltpu.VMEM((width, width), BF16),
            pltpu.VMEM((width, TILE), BF16),
            pltpu.VMEM((TILE, width), BF16),
            pltpu.SemaphoreType.DMA,
        ],
        compiler_params=pltpu.CompilerParams(vmem_limit_bytes=62 * 2**20),
        name="layer",
    )(lengths, task_of, task_tokens, x, grad_out, wqkv, wout, wup, wdn, vecs)


def pack_vectors(bias_q, bias_v, bias_out, bias_up, bias_down, gain_one, shift_one, gain_two, shift_two):
    width = bias_q.shape[0]
    rows = jnp.stack([bias_q, bias_v, bias_out, bias_down, gain_one, shift_one, gain_two, shift_two])
    tiles = jnp.pad(bias_up.reshape(-1, TILE), ((0, 0), (0, width - TILE)))
    rest = jnp.zeros((VEC_ROWS - rows.shape[0] - tiles.shape[0], width), BF16)
    return jnp.concatenate([rows, tiles, rest]).astype(F32)


def plain_body(
    tokens, grad_out, lengths, task_of, task_tokens, w_qkv, w_out, w_up, w_down,
    bias_q, bias_v, bias_out, bias_up, bias_down, gain_one, shift_one, gain_two, shift_two,
):
    gather = lambda a: lax.all_gather(a, "dp", axis=0, tiled=True)
    width = tokens.shape[2]
    chunks, tiles = width // BLOCK, w_up.shape[1] // TILE
    wqkv = gather(w_qkv).reshape(width, 3, chunks, BLOCK).transpose(2, 0, 1, 3)
    wqkv = wqkv.reshape(chunks, width, 3 * BLOCK)
    wup = gather(w_up).reshape(width, tiles, TILE).transpose(1, 0, 2)
    wdn = gather(w_down).reshape(tiles, TILE, width)
    vecs = pack_vectors(
        *(gather(a) for a in (bias_q, bias_v, bias_out, bias_up, bias_down, gain_one, shift_one, gain_two, shift_two))
    )
    act, input_grad, gqkv, gout, gup, gdn, gvec = plain_layer(
        lengths, task_of, task_tokens, tokens[0], grad_out[0], wqkv, gather(w_out), wup, wdn, vecs
    )
    gqkv = gqkv.reshape(chunks, width, 3, BLOCK).transpose(1, 2, 0, 3).reshape(width, 3 * width)
    gup = gup.transpose(1, 0, 2).reshape(width, -1)
    gdn = gdn.reshape(-1, width)
    vectors = [gvec[BQ], gvec[BV], gvec[BO], gvec[UP : UP + tiles, :TILE].reshape(-1), gvec[BD]]
    vectors += [gvec[G1], gvec[S1], gvec[G2], gvec[S2]]
    grads = [gqkv, gout, gup, gdn] + [a.astype(BF16) for a in vectors]
    shares = lax.psum_scatter(grads, "dp", scatter_dimension=0, tiled=True)
    summed = jax.tree.map(lambda a: a.astype(F32), lax.psum(shares, "grp"))
    return (act[None], input_grad[None], *summed)


MESH = pl.DeviceIdType.MESH


class Place:
    def __init__(self):
        z, d = lax.axis_index("grp"), lax.axis_index("dp")
        self.z, self.d = z, d
        self.core = lax.rem(d, 2)
        self.chip = d // 2
        x, y = lax.rem(self.chip, 2), d // 4
        self.d_core = d + 1 - 2 * self.core
        self.d_x = d + 2 - 4 * x
        self.d_y = d + 4 - 8 * y
        self.d_diag = self.d_x + 4 - 8 * y
        self.chip_x, self.chip_y, self.chip_diag = self.d_x // 2, self.d_y // 2, self.d_diag // 2
        self.odd = lax.rem(z, 2)
        self.on_z = (z + 1 - 2 * self.odd, d)
        self.on_core, self.on_x, self.on_y = ((z, e) for e in (self.d_core, self.d_x, self.d_y))
        self.outer = (z == 0) | (z == 3)
        self.inner = (z == 1) | (z == 2)
        self.to_inner = (1 + z // 3, d)
        self.to_outer = (3 * (z // 2), d)
        self.to_mid = (3 - z, d)


def remote(src, dst, sems, index, device):
    send, recv = sems
    return pltpu.make_async_remote_copy(
        src_ref=src, dst_ref=dst, send_sem=send.at[index], recv_sem=recv.at[index],
        device_id=device, device_id_type=MESH,
    )


class Gather:
    def __init__(self, here, full, sems):
        self.here, self.full, self.sems = here, full, sems
        self.count, rows, _ = full.shape
        self.rows = rows // 8
        self.once = (self.rows - 32) // 2
        self.span = self.rows - self.once

    def block(self, i, owner, start=0, rows=None):
        rows = self.rows if rows is None else rows
        at = pl.ds(pl.multiple_of(owner * self.rows + start, 16), rows)
        return self.full.at[i, at, :]

    def crossing(self, i, owner):
        return self.block(i, owner, self.here.odd * self.once, self.span)

    def half(self, i, owner, n):
        start = self.here.odd * self.once + 32 * n
        return self.block(i, owner, start, 32 if n == 0 else self.span - 32)

    def shared(self, i, owner, odd):
        return self.block(i, owner, odd * (self.rows - self.once), self.once)

    def copy(self, i, n):
        p = self.here
        part, device = (
            lambda: (self.crossing(i, p.d), p.on_x),
            lambda: (self.crossing(i, p.d), p.on_y),
            lambda: (self.block(i, p.d), p.on_core),
            lambda: (self.block(i, p.d_x), p.on_core),
            lambda: (self.half(i, p.d_x, 0), p.on_y),
            lambda: (self.block(i, p.d_y), p.on_core),
            lambda: (self.half(i, p.d_y, 1), p.on_x),
            lambda: (self.block(i, p.d_diag), p.on_core),
            lambda: (self.shared(i, p.d_x, p.odd), p.on_z),
            lambda: (self.shared(i, p.d_y, p.odd), p.on_z),
            lambda: (self.shared(i, p.d_diag, p.odd), p.on_z),
        )[n]()
        return remote(part, part, self.sems, (n, i), device)

    def landed(self, i, n):
        p = self.here
        flip = 1 - 2 * p.core
        part = (
            lambda: self.crossing(i, p.d_x),
            lambda: self.crossing(i, p.d_y),
            lambda: self.block(i, p.d_core),
            lambda: self.block(i, p.d_x + flip),
            lambda: self.half(i, p.d_diag, 0),
            lambda: self.block(i, p.d_y + flip),
            lambda: self.half(i, p.d_diag, 1),
            lambda: self.block(i, p.d_diag + flip),
            lambda: self.shared(i, p.d_x, 1 - p.odd),
            lambda: self.shared(i, p.d_y, 1 - p.odd),
            lambda: self.shared(i, p.d_diag, 1 - p.odd),
        )[n]()
        remote(part, part, self.sems, (n, i), p.on_core).wait_recv()

    def begin(self, i, *numbers):
        for n in numbers:
            self.copy(i, n).start()

    def start(self, i):
        self.begin(i, 0, 1, 2)

    def relay(self, i):
        self.landed(i, 0)
        self.begin(i, 4, 8)
        self.landed(i, 1)
        self.begin(i, 6, 9)

    def diag(self, i):
        self.landed(i, 4)
        self.landed(i, 6)
        self.begin(i, 10)

    def hand(self, i):
        self.landed(i, 8)
        self.begin(i, 3)
        self.landed(i, 9)
        self.begin(i, 5)
        self.landed(i, 10)
        self.begin(i, 7)

    def need(self, i):
        for n in (2, 3, 5, 7):
            self.landed(i, n)

    def drain(self):
        def step(i, _):
            for n in range(11):
                self.copy(i, n).wait_send()
            return 0

        lax.fori_loop(0, self.count, step, 0)


def added(*refs_at):
    total = refs_at[0].astype(F32)
    for value in refs_at[1:]:
        total = total + value.astype(F32)
    return total.astype(BF16)


class Reduce:
    STAGES = 7

    def __init__(self, here, bufs, sems):
        self.here, self.sems = here, sems
        (self.sums, self.from_core, self.half_x, self.half_y, self.from_x, self.from_y,
         self.run, self.from_outer, self.from_mid, self.total) = bufs
        self.count, self.rows, self.columns = self.total.shape
        self.slots, self.run_slots = self.sums.shape[0] - 1, self.run.shape[0]
        self.half_slots, self.side_slots = self.half_x.shape[0], self.from_x.shape[0]

    @staticmethod
    def buffers(count, rows, columns, slots, half_slots, run_slots):
        piece = (rows, columns)
        shapes = [(slots + 1, 4) + piece, (2, 4) + piece]
        shapes += [(half_slots, rows // 2, columns)] * 2 + [(run_slots,) + piece] * 2
        shapes += [(run_slots,) + piece, (run_slots,) + piece, (2,) + piece, (count,) + piece]
        return [pltpu.VMEM(shape, BF16) for shape in shapes]

    def mine(self, i):
        return 1 + lax.rem(i, self.slots)

    def copy(self, i, n):
        p, two, half = self.here, lax.rem(i, 2), self.rows // 2
        own = self.mine(i)
        at = lax.rem(i, self.run_slots)
        run, half_at = self.run.at[at], lax.rem(i, self.half_slots)
        src, dst, device = (
            lambda: (self.sums.at[0], self.from_core.at[two], p.on_core),
            lambda: (self.sums.at[own, p.chip_diag, :half], self.half_x.at[half_at], p.on_x),
            lambda: (self.sums.at[own, p.chip_diag, half:], self.half_y.at[half_at], p.on_y),
            lambda: (self.sums.at[own, p.chip_x], self.from_x.at[at], p.on_x),
            lambda: (self.sums.at[own, p.chip_y], self.from_y.at[at], p.on_y),
            lambda: (run, self.from_outer.at[at], p.to_inner),
            lambda: (run, self.from_mid.at[two], p.to_mid),
            lambda: (self.total.at[i], self.total.at[i], p.to_outer),
        )[n]()
        return remote(src, dst, self.sems, (n, i), device)

    def stage_0(self, i, value):
        own, rows = self.mine(i), self.rows
        for owner in range(8):
            same = 1 - lax.rem(self.here.core + owner, 2)
            self.sums[same * own, owner // 2] = value[owner * rows : (owner + 1) * rows]
        self.copy(i, 0).start()

    def stage_1(self, i):
        own, two = self.mine(i), lax.rem(i, 2)
        done = self.copy(i, 0)
        done.wait_recv()
        done.wait_send()
        order = (self.here.chip_diag, self.here.chip_x, self.here.chip_y, self.here.chip)
        for n, chip in enumerate(order):
            self.sums[own, chip] = added(self.sums[own, chip], self.from_core[two, chip])
            if n == 0:
                self.copy(i, 1).start()
                self.copy(i, 2).start()

    def stage_2(self, i):
        p, own, half = self.here, self.mine(i), self.rows // 2
        at = lax.rem(i, self.half_slots)
        self.copy(i, 1).wait_recv()
        self.copy(i, 2).wait_recv()
        self.sums[own, p.chip_y, :half] = added(self.sums[own, p.chip_y, :half], self.half_x[at])
        self.copy(i, 4).start()
        self.sums[own, p.chip_x, half:] = added(self.sums[own, p.chip_x, half:], self.half_y[at])
        self.copy(i, 3).start()

    def stage_3(self, i):
        p, own, at = self.here, self.mine(i), lax.rem(i, self.run_slots)
        self.copy(i, 3).wait_recv()
        self.copy(i, 4).wait_recv()
        self.run[at] = added(self.sums[own, p.chip], self.from_x[at], self.from_y[at])
        for n in (1, 2, 3, 4):
            self.copy(i, n).wait_send()
        pl.when(p.outer)(lambda: self.copy(i, 5).start())

    def stage_4(self, i):
        def work():
            self.copy(i, 5).wait_recv()
            at = lax.rem(i, self.run_slots)
            self.run[at] = added(self.run[at], self.from_outer[at])
            self.copy(i, 6).start()

        pl.when(self.here.inner)(work)

    def stage_5(self, i):
        def work():
            self.copy(i, 6).wait_recv()
            self.total[i] = added(self.run[lax.rem(i, self.run_slots)], self.from_mid[lax.rem(i, 2)])
            self.copy(i, 7).start()

        pl.when(self.here.inner)(work)

    def stage_6(self, i):
        def finish_inner():
            self.copy(i, 6).wait_send()
            self.copy(i, 7).wait_send()

        def finish_outer():
            self.copy(i, 5).wait_send()
            self.copy(i, 7).wait_recv()

        pl.when(self.here.inner)(finish_inner)
        pl.when(self.here.outer)(finish_outer)

    def stage(self, s, i):
        getattr(self, "stage_%d" % s)(i)

    def guarded(self, s, i):
        if isinstance(i, int):
            if 0 <= i < self.count:
                self.stage(s, i)
            return
        pl.when((i >= 0) & (i < self.count))(lambda: self.stage(s, i))


class Fused:
    def __init__(self, here, ins, outs, g, c):
        self.here, self.ins, self.outs, self.g, self.c = here, ins, outs, g, c
        self.gather = {
            kind: Gather(here, g[kind], (c["g_send_" + kind], c["g_recv_" + kind])) for kind in "qud"
        }
        self.reduce = {
            kind: Reduce(here, c["r_" + kind], (c["r_send_" + kind], c["r_recv_" + kind]))
            for kind in "qud"
        }

    def gather_step(self, name, item):
        def tile():
            for kind in "ud":
                getattr(self.gather[kind], name)(item - 4)

        def chunk():
            getattr(self.gather["q"], name)(item)

        if isinstance(item, int):
            if 0 <= item < 4:
                chunk()
            elif 4 <= item < 10:
                tile()
        else:
            pl.when((item >= 0) & (item < 4))(chunk)
            pl.when((item >= 4) & (item < 10))(tile)

    def gather_point(self, k):
        if not isinstance(k, int) or k >= 3:
            self.gather_step("hand", k - 2)
        self.gather_step("relay", k)
        self.gather_step("start", k + 2)
        self.gather_step("diag", k - 1)

    def hidden_point(self, p):
        for stage, lag in ((6, 7), (5, 6), (4, 5), (3, 4), (1, 1), (2, 2)):
            for kind in "ud":
                self.reduce[kind].guarded(stage, p - lag)

    def greet(self):
        p, barrier = self.here, pltpu.get_barrier_semaphore()
        for step in range(1, 8):
            pl.semaphore_signal(
                barrier, inc=1, device_id=(p.z, lax.rem(p.d + step, 8)), device_id_type=MESH
            )
        for step in range(1, 4):
            pl.semaphore_signal(
                barrier, inc=1, device_id=(lax.rem(p.z + step, 4), p.d), device_id_type=MESH
            )
        pl.semaphore_wait(barrier, 10)

    def vector_copy(self, kind, step):
        p, c = self.here, self.c
        sems = (c["v_send"], c["v_recv"])
        if kind == 2:
            device = (lax.rem(p.z + step, 4), p.d)
            return remote(c["vz"].at[p.z], c["vz"].at[p.z], sems, (kind, step), device)
        device = (p.z, lax.rem(p.d + step, 8))
        if kind == 0:
            return remote(self.ins["vec"], c["vfull"].at[p.d], sems, (kind, step), device)
        return remote(c["vpack"].at[device[1]], c["vin"].at[step], sems, (kind, step), device)

    def vector_landed(self, kind, step):
        p, c = self.here, self.c
        sems = (c["v_send"], c["v_recv"])
        if kind == 2:
            part = c["vz"].at[lax.rem(p.z + 4 - step, 4)]
        elif kind == 0:
            part = c["vfull"].at[lax.rem(p.d + 8 - step, 8)]
        else:
            part = c["vin"].at[step]
        remote(part, part, sems, (kind, step), p.on_core).wait_recv()

    def own_copies(self):
        p, ins, g, sem = self.here, self.ins, self.g, self.c["own"]
        rows, width = ins["out"].shape
        parts = [[], [], [], [], []]
        at = pl.ds(pl.multiple_of(p.d * rows, 16), rows)
        for j in range(3):
            for part in range(3):
                src = ins["qkv"].at[:, pl.ds(part * width + j * BLOCK, BLOCK)]
                parts[j].append((src, g["q"].at[j, at, pl.ds(part * BLOCK, BLOCK)]))
        parts[3].append((ins["out"], g["q"].at[3, at, :]))
        for t in range(6):
            down = pl.ds(pl.multiple_of(p.d * 64, 16), 64)
            parts[4].append((ins["down"].at[pl.ds(64 * t, 64), :], g["d"].at[t, down, :]))
        copies = []
        for n, part in enumerate(parts):
            copies.append([pltpu.make_async_copy(src, dst, sem.at[n]) for src, dst in part])
        return copies

    def up_copies(self, room):
        rows = self.ins["up"].shape[0]
        return [
            pltpu.make_async_copy(
                self.ins["up"].at[:, pl.ds(1024 * b, 1024)],
                room.at[pl.ds(rows * b, rows), :],
                self.c["own"].at[5],
            )
            for b in range(3)
        ]

    def place_up(self, room):
        rows = self.ins["up"].shape[0]
        at = pl.ds(pl.multiple_of(self.here.d * rows, 16), rows)

        def piece(owner, t):
            start = 384 * owner + 64 * t
            block, off = start // 1024, start % 1024
            return room[block * rows : (block + 1) * rows, off : off + 64]

        for t in range(6):
            for pair in range(4):
                both = jnp.concatenate([piece(2 * pair, t), piece(2 * pair + 1, t)], axis=1)
                self.g["u"][t, at, 128 * pair : 128 * (pair + 1)] = both

    def spread_vectors(self, vecs):
        vfull = self.c["vfull"]
        vecs[...] = jnp.zeros_like(vecs)
        rows = self.ins["out"].shape[0]
        for owner in range(8):
            vecs[0:8, rows * owner : rows * (owner + 1)] = vfull[owner, 0:8, :rows]
            vecs[8:14, 64 * owner : 64 * (owner + 1)] = vfull[owner, 8:14, :64]

    def pack_vectors(self, gvec):
        vpack = self.c["vpack"]
        vpack[...] = jnp.zeros_like(vpack)
        rows = self.ins["out"].shape[0]
        for owner in range(8):
            vpack[owner, 0:8, :rows] = gvec[0:8, rows * owner : rows * (owner + 1)]
            vpack[owner, 8:14, :64] = gvec[8:14, 64 * owner : 64 * (owner + 1)]


def fused_body(comm, lengths, task_of, task_tokens, hbm_x, hbm_grad, act, input_grad, vecs, s):
    here, c, g = comm.here, comm.c, comm.g
    gq, gu, gd = (comm.gather[kind] for kind in "qud")
    rq, ru, rd = (comm.reduce[kind] for kind in "qud")
    wq, wup, wdn = g["q"], g["u"], g["d"]
    wout = wq.at[3]
    length_s = lengths[0]
    weight_s = task_weight(task_of, task_tokens)
    get_x = pltpu.make_async_copy(hbm_x, s.x, s.local.at[2])
    get_grad = pltpu.make_async_copy(hbm_grad, s.x, s.local.at[3])
    get_x_again = pltpu.make_async_copy(hbm_x, s.x, s.local.at[4])
    own = comm.own_copies()
    ups = comm.up_copies(s.o_t)
    own_vec = pltpu.make_async_copy(comm.ins["vec"], c["vfull"].at[here.d], c["own"].at[6])
    for copy in own[0] + [own_vec] + own[1] + own[2] + [get_x] + ups + own[3] + own[4]:
        copy.start()
    s.gvec[...] = jnp.zeros_like(s.gvec)
    s.da2[...] = jnp.zeros_like(s.da2)
    comm.greet()
    for step in range(1, 8):
        comm.vector_copy(0, step).start()
    for j in range(2):
        for copy in own[j]:
            copy.wait()
        gq.start(j)
    for copy in own[2]:
        copy.wait()
    own_vec.wait()
    for step in range(1, 8):
        comm.vector_landed(0, step)
    comm.spread_vectors(vecs)
    get_x.wait()
    norm_one_phase(s.x, vecs, s.a1, s.x2)
    get_grad.start()
    comm.gather_point(0)
    for copy in ups:
        copy.wait()
    comm.place_up(s.o_t)
    for copy in own[3] + own[4]:
        copy.wait()
    comm.gather_point(1)
    get_grad.wait()
    branch_phase(s.x, length_s, weight_s, s.g_f, s.gvec)
    gq.hand(0)

    def forward(j, _):
        gq.need(j)
        qkv_phase(j, s.a1, wq, vecs, s.k, s.v, s.q_t, s.k_t, s.v_t)
        comm.gather_step("relay", 2 * j + 2)
        comm.gather_step("start", 2 * j + 4)
        comm.gather_step("diag", 2 * j + 1)
        pl.when(j > 0)(lambda: comm.gather_step("hand", 2 * j))

        def pair(n, _):
            attend_pair(2 * j + n, length_s, s.k, s.q_t, s.v_t, s.o_t, s.lse)
            pl.when(n == 0)(lambda: comm.gather_point(2 * j + 3))
            return 0

        return lax.fori_loop(0, 2, pair, 0)

    lax.fori_loop(0, 3, forward, 0)
    gq.need(3)
    norm_two_phase(s.o_t, wout, vecs, s.x2, s.a2, s.out_acc)
    comm.gather_point(8)
    hr, gu_tile = s.work.at[:, :TILE], s.work.at[:, TILE:]

    def hidden(t, _):
        gu.need(t)
        gd.need(t)
        hidden_tile(t, s.a2, s.g_f, wup, wdn, vecs, s.out_acc, s.da2, hr, gu_tile, s.gvec)
        comm.gather_point(9 + t)
        comm.hidden_point(t)
        ru.stage_0(t, tn(s.a2[...], gu_tile[...]).astype(BF16))
        rd.stage_0(t, tn(hr[...], s.g_f[...]).astype(BF16))
        return 0

    lax.fori_loop(0, 6, hidden, 0)

    norm_two_back(s.x, length_s, weight_s, s.x2, s.da2, vecs, s.a2, s.gvec, s.out_acc, s.g_f)
    get_x_again.start()
    act_copy = pltpu.make_async_copy(s.g_f, act, s.local.at[0])
    act_copy.start()
    comm.hidden_point(6)
    rq.stage_0(0, nn(s.o_t[...], s.a2[...]).astype(BF16))
    g_o_t = s.v_t
    attended_back(wout, s.a2, s.o_t, g_o_t, s.delta)
    da1 = s.out_acc
    da1[...] = jnp.zeros_like(da1)
    dqkv = s.work.at[:, : 3 * BLOCK]

    def backward(j, _):
        def pair(n, _):
            attend_back_pair(
                2 * j + n, s.k, s.v, s.q_t, s.k_t, g_o_t, s.lse, s.delta,
                s.dk_t, s.dv_t, dqkv, s.gvec,
            )
            comm.hidden_point(7 + 2 * j + n)

            def even():
                rq.guarded(6, j - 3)
                rq.guarded(4, j - 2)
                rq.stage(1, j)

            def odd():
                rq.guarded(5, j - 2)
                rq.guarded(3, j - 1)
                rq.stage(2, j)

            pl.when(n == 0)(even)
            pl.when(n == 1)(odd)
            return 0

        lax.fori_loop(0, 2, pair, 0)
        rq.stage_0(j + 1, tn(s.a1[...], dqkv[...]).astype(BF16))
        for m in range(s.x.shape[0] // BLOCK):
            at = slice(m * BLOCK, (m + 1) * BLOCK)
            da1[at, :] += nt(dqkv[at, :], wq[j])
        return 0

    lax.fori_loop(0, 3, backward, 0)
    get_x_again.wait()
    rq.stage(6, 0)
    rq.stage(4, 1)
    rq.stage(1, 3)
    norm_one_back(s.x, s.da2, da1, vecs, s.gvec, s.a1)
    grad_copy = pltpu.make_async_copy(s.a1, input_grad, s.local.at[1])
    grad_copy.start()
    comm.pack_vectors(s.gvec)
    for step in range(1, 8):
        comm.vector_copy(1, step).start()
    rq.stage(5, 1)
    rq.stage(3, 2)
    rq.stage(2, 3)
    outs = comm.outs
    rows = comm.ins["out"].shape[0]
    width = s.x.shape[1]
    x2 = s.x2
    x2[:rows, :] = rq.total[0].astype(F32)
    copies = [pltpu.make_async_copy(x2.at[pl.ds(0, rows), :], outs["out"], s.local.at[5])]
    copies[0].start()
    for t in range(6):
        x2[rows + 64 * t : rows + 64 * (t + 1), :] = rd.total[t].astype(F32)
    copies.append(pltpu.make_async_copy(x2.at[pl.ds(rows, 384), :], outs["down"], s.local.at[6]))
    copies[1].start()
    base = rows + 384
    for group in range(24):
        owner, t = group // 3, 2 * (group % 3)
        lanes = slice(64 * owner, 64 * (owner + 1))
        both = jnp.concatenate([ru.total[t, :, lanes], ru.total[t + 1, :, lanes]], axis=1)
        at, off = base + rows * (group // 6), 128 * (group % 6)
        x2[at : at + rows, off : off + 128] = both.astype(F32)
    for b in range(4):
        copies.append(
            pltpu.make_async_copy(
                x2.at[pl.ds(base + rows * b, rows), :],
                outs["up"].at[:, pl.ds(width * b, width)],
                s.local.at[7 + b],
            )
        )
        copies[-1].start()
    for step in range(1, 8):
        comm.vector_landed(1, step)
    share = c["vpack"][here.d]
    for step in range(1, 8):
        share = share + c["vin"][step]
    c["vz"][here.z] = share
    for step in range(1, 4):
        comm.vector_copy(2, step).start()
    rq.stage(6, 1)
    rq.stage(4, 2)
    rq.stage(3, 3)

    def out_qkv(j):
        for part in range(3):
            da1[part * rows : (part + 1) * rows, j * BLOCK : (j + 1) * BLOCK] = rq.total[
                j + 1, :, part * BLOCK : (part + 1) * BLOCK
            ].astype(F32)

    out_qkv(0)
    rq.stage(5, 2)
    rq.stage(4, 3)
    rq.stage(6, 2)
    out_qkv(1)
    for step in range(1, 4):
        comm.vector_landed(2, step)
    vz = c["vz"]
    outs["vec"][...] = (vz[0] + vz[1]) + (vz[2] + vz[3])
    gq.drain()
    gu.drain()
    gd.drain()
    for kind, count in ((0, 8), (1, 8), (2, 4)):
        for step in range(1, count):
            comm.vector_copy(kind, step).wait_send()
    rq.stage(5, 3)
    rq.stage(6, 3)
    out_qkv(2)
    for part in range(3):
        copies.append(
            pltpu.make_async_copy(
                da1.at[pl.ds(part * rows, rows), :],
                outs["qkv"].at[:, pl.ds(width * part, width)],
                s.local.at[11 + part],
            )
        )
        copies[-1].start()
    act_copy.wait()
    grad_copy.wait()
    for copy in copies:
        copy.wait()


def fused_layer(lengths, task_of, task_tokens, x, grad_out, w_qkv, w_out, w_up, w_down, vec):
    length, width = x.shape
    rows = w_out.shape[0]
    shapes = layer_scratch(length, width)
    shapes["x"] = pltpu.VMEM((length, width), BF16)
    shapes["vecs"] = pltpu.VMEM((VEC_ROWS, width), F32)
    shapes["local"] = pltpu.SemaphoreType.DMA((14,))
    full = {
        "q": pltpu.VMEM((4, width, width), BF16),
        "u": pltpu.VMEM((6, width, TILE), BF16),
        "d": pltpu.VMEM((6, TILE, width), BF16),
    }
    comm_shapes = {
        "own": pltpu.SemaphoreType.DMA((7,)),
        "v_send": pltpu.SemaphoreType.DMA((3, 8)),
        "v_recv": pltpu.SemaphoreType.DMA((3, 8)),
        "vfull": pltpu.VMEM((8, VEC_ROWS, 128), F32),
        "vpack": pltpu.VMEM((8, VEC_ROWS, 128), F32),
        "vin": pltpu.VMEM((8, VEC_ROWS, 128), F32),
        "vz": pltpu.VMEM((4, VEC_ROWS, 128), F32),
    }
    for kind, count in (("q", 4), ("u", 6), ("d", 6)):
        for name in ("g_send_", "g_recv_"):
            comm_shapes[name + kind] = pltpu.SemaphoreType.DMA((11, count))
        for name in ("r_send_", "r_recv_"):
            comm_shapes[name + kind] = pltpu.SemaphoreType.DMA((8, count))
    sums = {
        "q": Reduce.buffers(4, rows, width, 2, 2, 2),
        "u": Reduce.buffers(6, rows, TILE, 4, 4, 3),
        "d": Reduce.buffers(6, 64, width, 4, 4, 3),
    }
    names, comm_names = tuple(shapes), tuple(comm_shapes)
    scratch = list(shapes.values()) + list(full.values()) + list(comm_shapes.values())
    for kind in "qud":
        scratch += sums[kind]

    def kernel(*refs):
        refs = list(refs)
        take = lambda n: [refs.pop(0) for _ in range(n)]
        lens, of, tokens, hbm_x, hbm_grad = take(5)
        ins = dict(zip(("qkv", "out", "up", "down", "vec"), take(5)))
        act, input_grad = take(2)
        outs = dict(zip(("qkv", "out", "up", "down", "vec"), take(5)))
        s = Named(names, take(len(names)))
        g = dict(zip("qud", take(3)))
        c = dict(zip(comm_names, take(len(comm_names))))
        for kind in "qud":
            c["r_" + kind] = take(10)
        comm = Fused(Place(), ins, outs, g, c)
        fused_body(comm, lens, of, tokens, hbm_x, hbm_grad, act, input_grad, s.vecs, s)

    smem = pl.BlockSpec(memory_space=pltpu.SMEM)
    vmem = pl.BlockSpec(memory_space=pltpu.VMEM)
    hbm = pl.BlockSpec(memory_space=pl.ANY)
    like = lambda a: jax.ShapeDtypeStruct(a.shape, F32)
    return pl.pallas_call(
        kernel,
        out_shape=(
            jax.ShapeDtypeStruct(x.shape, BF16), jax.ShapeDtypeStruct(x.shape, BF16),
            like(w_qkv), like(w_out), like(w_up), like(w_down), like(vec),
        ),
        in_specs=[smem] * 3 + [hbm] * 6 + [vmem],
        out_specs=(hbm,) * 6 + (vmem,),
        scratch_shapes=scratch,
        compiler_params=pltpu.CompilerParams(
            vmem_limit_bytes=63 * 2**20, collective_id=0, has_side_effects=True
        ),
        name="layer",
    )(lengths, task_of, task_tokens, x, grad_out, w_qkv, w_out, w_up, w_down, vec)


def fused_shards(
    tokens, grad_out, lengths, task_of, task_tokens, w_qkv, w_out, w_up, w_down,
    bias_q, bias_v, bias_out, bias_up, bias_down, gain_one, shift_one, gain_two, shift_two,
):
    rows = w_out.shape[0]
    eight = jnp.stack([bias_q, bias_v, bias_out, bias_down, gain_one, shift_one, gain_two, shift_two])
    up = bias_up.reshape(6, 64)
    vec = jnp.concatenate(
        [
            jnp.pad(eight, ((0, 0), (0, 128 - rows))),
            jnp.pad(up, ((0, VEC_ROWS - 8 - 6), (0, 64))),
        ]
    ).astype(F32)
    act, input_grad, gqkv, gout, gup, gdn, gvec = fused_layer(
        lengths, task_of, task_tokens, tokens[0], grad_out[0], w_qkv, w_out, w_up, w_down, vec
    )
    line = lambda n: gvec[n, :rows]
    return (
        act[None], input_grad[None], gqkv, gout, gup, gdn, line(BQ), line(BV), line(BO),
        gvec[UP : UP + 6, :64].reshape(-1), line(BD), line(G1), line(S1), line(G2), line(S2),
    )


def solution(mesh):
    rows = P(("grp", "dp"), None, None)
    each = P(("grp", "dp"))
    matrix, vector = P("dp", None), P("dp")
    in_specs = (rows, rows, each, each, P()) + (matrix,) * 4 + (vector,) * 9
    out_specs = (rows, rows) + (matrix,) * 4 + (vector,) * 9
    small = mesh.shape["dp"] == 8 and mesh.shape["grp"] == 4
    body = fused_shards if small else plain_body
    return jax.shard_map(body, mesh=mesh, in_specs=in_specs, out_specs=out_specs, check_vma=False)
```
